32 devices in a mesh: dom: 2 (over x), wide: 8 (over z, y), grad: 2 (over core).
Axes of the slice: x: 2, y: 2, z: 4, core: 2. Of those that a mesh axis runs over, the one named last changes fastest.
Arguments:
- activations: bfloat16 [16, 2048, 2048], P(('dom', 'wide'), 'grad'), parts along dimension 0, may hold values from -3 to 3
- inverse: bfloat16 [16, 2048, 2048], P(('dom', 'wide'), 'grad'), parts along dimension 0, as said below
- gradients: bfloat16 [16, 2048, 384], P(('dom', 'wide'), 'grad'), parts along dimension 0, may hold values from -6 to 6
- matching: int32 [16], P('dom'), parts along dimension 0, may hold values from 0 to 7, each once
- live_rows: int32 [16], P('dom'), parts along dimension 0, may hold values from 1 to 2048, 12288 in all
Outputs:
- preconditioned: bfloat16 [16, 2048, 384], P(('dom', 'wide'), 'grad'), parts along dimension 0
The draws below stay inside these ranges and needn't reach their ends.
There are 2 independent parts, one for each index of `dom`. The reference program is written for one: setup_inputs(seed, part) draws one part's arguments, and reference() takes and returns one part's arrays. A program takes and returns all parts, laid end to end along the dimension named above; each array names one. Nothing has to cross between parts.
Inputs may be any that keep to these rules, and one draw needn't show every extreme that they name: matching names every index of wide once; inverse tile s is used for the tile of index matching[s]. The live rows of tile t are its first live_rows[t] rows; some tile has all 2048. `inverse`: symmetric.
All inputs are finite; a program needn't handle non-finite values.
Results may differ from the reference program's by a relative error of at most 0.0059.
Values may be sent and summed in bfloat16 or wider, within the bound.
A program may use at most 128 MiB of HBM per device.

```python
import math
import jax
import jax.numpy as jnp
import numpy as np
from jax import lax

TILE = 2048
COLS = 384
ROWS = 2048
N_WIDE = 8


def draw_inverse(key, part):
    key = jax.random.fold_in(key, 7)
    noise_key, diag_key = jax.random.split(key)
    noise = jax.random.normal(noise_key, (N_WIDE, TILE, TILE), jnp.float32)
    diag_vals = 0.3 * 2.0 ** jax.random.uniform(diag_key, (N_WIDE, TILE), jnp.float32)
    offdiag = (noise + jnp.swapaxes(noise, 1, 2)) * (0.18 / math.sqrt(TILE))
    identity = jnp.eye(TILE, dtype=jnp.float32)
    return (offdiag + diag_vals[:, :, None] * identity[None, :, :]).astype(jnp.bfloat16)


def level_of(own_key, shape, pieces, smallest, top_value):
    factor_of = 1.0
    for position, parts in pieces:
        heights = jax.random.uniform(jax.random.fold_in(jax.random.fold_in(own_key, 6), position), (parts,), jnp.float32, smallest / len(pieces), top_value / len(pieces))
        factor_of = factor_of * jnp.repeat(jnp.exp(heights), shape[position] // parts).reshape((-1,) + (1,) * (len(shape) - 1 - position))
    return factor_of


def length_profile(amount, total, reach, slope):
    portions = [(1 << 20) // math.isqrt(grade ** slope) + 1 for grade in range(2, amount + 1)]
    rest, counts = total - reach - (amount - 1), [1] * (amount - 1)
    while rest > 0:
        free = [i for i in range(amount - 1) if counts[i] < reach]
        pool, budget = sum([portions[i] for i in free]), rest
        for i in free:
            addition = min(reach - counts[i], max(1, budget * portions[i] // pool), rest)
            counts[i] = counts[i] + addition
            rest = rest - addition
    return np.array([reach] + counts)


def uneven(stream_key, number_of, total, bound, skew):
    if number_of == 2:
        one = jax.random.randint(stream_key, (), max(1, total - bound), min(bound, total - 1) + 1)
        return jnp.stack([one, total - one])
    tallies = jnp.asarray(length_profile(number_of, total, bound, skew), jnp.int32)
    couples = (number_of - 1) // 2
    donor, sink = tallies[1:1 + 2 * couples:2], tallies[2:2 + 2 * couples:2]
    margin = jnp.minimum(donor - 1, bound - sink)
    shifted = jax.random.randint(jax.random.fold_in(stream_key, 1), (couples,), 0, 1 << 20) % (margin + 1)
    tallies = tallies.at[1:1 + 2 * couples:2].set(donor - shifted).at[2:2 + 2 * couples:2].set(sink + shifted)
    return tallies[jax.random.permutation(jax.random.fold_in(stream_key, 2), number_of)]


def scatter_about(stream_key, dims, width, limit, cuts=(), kind=jnp.bfloat16):
    result = width * jax.random.normal(stream_key, dims, jnp.float32)
    if cuts:
        result = result * level_of(stream_key, dims, cuts, -0.22, 0.18)
    return jnp.clip(result, -limit, limit).astype(kind)


def setup_inputs(seed: int = 0, part: int = 0) -> dict:
    streams_of = jax.random.split(jax.random.key(seed), 6)
    own_keys = jax.random.split(jax.random.fold_in(streams_of[5], part), 6)
    return {
        "activations": scatter_about(own_keys[0], (N_WIDE, ROWS, TILE), 0.5, 3.0, ((0, 8), (1, 2))),
        "inverse": draw_inverse(jax.random.fold_in(jax.random.fold_in(streams_of[5], part), 71), part),
        "gradients": scatter_about(own_keys[2], (N_WIDE, TILE, COLS), 1.0, 6.0, ((0, 8), (1, 2))),
        "matching": jax.random.permutation(own_keys[3], N_WIDE).astype(jnp.int32),
        "live_rows": uneven(own_keys[4], N_WIDE, 3 * N_WIDE * ROWS // 4, ROWS, 1).astype(jnp.int32),
    }


DAMPING = 1.0


def reference(activations, inverse, gradients, matching, live_rows):
    places = jnp.arange(N_WIDE, dtype=jnp.int32)
    sources = jnp.sum(jnp.where(matching[None, :] == places[:, None], places[None, :], 0), axis=1).astype(jnp.int32)
    row_index = jnp.arange(ROWS, dtype=jnp.int32)
    identity = jnp.eye(TILE, dtype=jnp.float32)

    def per_tile(tile_index):
        tile_rows = activations[tile_index]
        inverse_tile = inverse[sources[tile_index]]
        grad_tile = gradients[tile_index]
        row_count = live_rows[tile_index]
        masked = jnp.where((row_index < row_count)[:, None], tile_rows, jnp.zeros_like(tile_rows))
        sums = jnp.dot(tile_rows.T, masked, preferred_element_type=jnp.float32)
        damped = (sums / row_count.astype(jnp.float32) + DAMPING * identity).astype(jnp.bfloat16)
        first_sum = jnp.dot(inverse_tile, grad_tile, preferred_element_type=jnp.float32)
        first_round = first_sum.astype(jnp.bfloat16)
        curvature = jnp.dot(damped, first_round, preferred_element_type=jnp.float32).astype(jnp.bfloat16)
        correction = jnp.dot(inverse_tile, curvature, preferred_element_type=jnp.float32)
        return (2.0 * first_sum - correction).astype(jnp.bfloat16)

    return lax.map(per_tile, places)
```

```python
import jax
import jax.numpy as jnp
from jax import lax
from jax.sharding import PartitionSpec as P

DAMPING = 1.0


def regroup(stacked, destination, groups):
    grouped = stacked.reshape((groups, stacked.shape[0] // groups) + stacked.shape[1:])
    return jnp.take(grouped, destination, axis=0).reshape(stacked.shape)


def product_step(matrix, shard_rows):
    return jnp.dot(matrix, shard_rows, preferred_element_type=jnp.float32)


def build_factor(tile_rows, row_count):
    core_index = lax.axis_index("grad")
    tile_order = tile_rows.shape[1]
    half_rows = tile_order // lax.axis_size("grad")
    live_count = row_count.astype(jnp.float32)
    shard_rows = lax.all_gather(tile_rows, "grad", axis=0, tiled=True)
    keep_rows = jnp.arange(shard_rows.shape[0], dtype=jnp.int32) < row_count
    masked = jnp.where(keep_rows[:, None], shard_rows, jnp.zeros_like(shard_rows))
    columns = lax.dynamic_slice_in_dim(shard_rows, core_index * half_rows, half_rows, 1)
    factor = jnp.einsum("rh,rc->hc", columns, masked, preferred_element_type=jnp.float32)
    diagonal = (core_index * half_rows + jnp.arange(half_rows, dtype=jnp.int32))[
        :, None
    ] == jnp.arange(tile_order, dtype=jnp.int32)[None, :]
    return (factor / live_count + jnp.where(diagonal, DAMPING, 0.0)).astype(jnp.bfloat16)


def first_product(inverse_rows, grad_rows):
    return product_step(inverse_rows, lax.all_gather(grad_rows, "grad", axis=0, tiled=True))


def curvature_product(damped, first_round):
    return product_step(damped, lax.all_gather(first_round, "grad", axis=0, tiled=True)).astype(
        jnp.bfloat16
    )


def correction_product(inverse_rows, curvature):
    return product_step(inverse_rows, lax.all_gather(curvature, "grad", axis=0, tiled=True))


def precondition(inverse_rows, tile_rows, grad_rows, row_count):
    damped = build_factor(tile_rows, row_count)
    first_sum = first_product(inverse_rows, grad_rows)
    curvature = curvature_product(damped, first_sum.astype(jnp.bfloat16))
    correction = correction_product(inverse_rows, curvature)
    return (2.0 * first_sum - correction).astype(jnp.bfloat16)


def pack(rows):
    core = lax.axis_index("grad")
    half = rows.shape[0]
    step = half // 8
    square = lax.dynamic_slice_in_dim(rows, core * half, half, 1)
    other = lax.dynamic_slice_in_dim(rows, (1 - core) * half, half, 1)
    folded = []
    for i in range(4):
        j = 7 - i
        folded.append(square[i * step : (i + 1) * step, i * step :])
        folded.append(square[j * step : (j + 1) * step, j * step :])
    flat = [piece.reshape(piece.shape[0], -1, 128).swapaxes(0, 1).reshape(-1, 128) for piece in folded]
    quarter = half // 2
    for h in range(2):
        block = lax.dynamic_slice_in_dim(
            other[h * quarter : (h + 1) * quarter], (h ^ core) * quarter, quarter, 1
        )
        flat.append(block.reshape(quarter, -1, 128).swapaxes(0, 1).reshape(-1, 128))
    return jnp.concatenate(flat, axis=0)


def unpack(flat, half):
    core = lax.axis_index("grad")
    step = half // 8
    quarter = half // 2
    at = 0

    def take(height, width):
        nonlocal at
        count = height * width // 128
        piece = flat[at : at + count]
        at += count
        return piece.reshape(width // 128, height, 128).swapaxes(0, 1).reshape(height, width)

    strips = [None] * 8
    for i in range(4):
        for k in (i, 7 - i):
            strips[k] = jnp.pad(take(step, half - k * step), ((0, 0), (k * step, 0)))
    upper = jnp.concatenate(strips, axis=0)
    block = jnp.arange(half, dtype=jnp.int32) // step
    square = jnp.where(block[:, None] <= block[None, :], upper, upper.T)
    own = [take(quarter, quarter) for _ in range(2)]
    size = lax.axis_size("grad")
    came = lax.ppermute(jnp.stack(own), "grad", [(c, (c + 1) % size) for c in range(size)])
    turned = [came[0].T, came[1].T]
    first = core == 0
    missing = [jnp.where(first, turned[1], turned[0]), jnp.where(first, turned[0], turned[1])]
    rows = []
    for h in range(2):
        left_own = first if h == 0 else jnp.logical_not(first)
        left = jnp.where(left_own, own[h], missing[h])
        right = jnp.where(left_own, missing[h], own[h])
        rows.append(jnp.concatenate([left, right], axis=1))
    other = jnp.concatenate(rows, axis=0)
    return jnp.concatenate(
        [jnp.where(first, square, other), jnp.where(first, other, square)], axis=1
    )


def per_device(activations, inverse, gradients, matching, live_rows):
    wide_size = lax.axis_size("wide")
    position = lax.axis_index("wide")
    places = jnp.arange(wide_size, dtype=jnp.int32)
    sources = jnp.sum(jnp.where(matching[None, :] == places[:, None], places[None, :], 0), axis=1)
    packed = pack(inverse[0])
    count = packed.shape[0]
    full = -(-count // (16 * wide_size)) * 16 * wide_size
    packed = jnp.pad(packed, ((0, full - count), (0, 0)))
    spread = lax.all_to_all(packed, "wide", split_axis=0, concat_axis=0, tiled=True)
    moved = lax.all_to_all(
        regroup(spread, sources, wide_size), "wide", split_axis=0, concat_axis=0, tiled=True
    )
    settled = unpack(moved, inverse.shape[1])
    result = precondition(settled, activations[0], gradients[0], live_rows[position])
    return result[None]


def solution(mesh):
    return jax.shard_map(
        per_device,
        mesh=mesh,
        in_specs=(
            P(("dom", "wide"), "grad", None),
            P(("dom", "wide"), "grad", None),
            P(("dom", "wide"), "grad", None),
            P("dom"),
            P("dom"),
        ),
        out_specs=P(("dom", "wide"), "grad", None),
        check_vma=False,
    )
```

```python
import functools

import jax
import jax.numpy as jnp
from jax import lax
from jax.experimental import pallas as pl
from jax.experimental.pallas import tpu as pltpu
from jax.sharding import PartitionSpec as P

DAMPING = 1.0
LANES = 128
CHUNKS = 4
MESH = pl.DeviceIdType.MESH


def dot(a, b):
    return jnp.dot(a, b, preferred_element_type=jnp.float32)


def kernel(
    n, half, cols, part,
    sources, live, act, inv, grad, out,
    packed, stage, moved, o_in, a_own, a_oth, lhs_t, m_own, m_oth,
    s_d, s_o, g_own, g_oth, first, acc, f_own, f_oth, c_own, c_oth,
    *rest,
):
    arrived = rest[:CHUNKS]
    (pack_sem, load_sem, send1, recv1, send2, recv2,
     send_a, recv_a, send_g, recv_g, send_o, recv_o, send_f, recv_f, send_c, recv_c) = rest[CHUNKS:]
    me = lax.axis_index("wide")
    core = lax.axis_index("grad")
    mate = 1 - core
    quarter = half // 2
    blocks = half // LANES
    o_rows = 2 * quarter * (quarter // LANES)

    def base(k):
        return o_rows + LANES * (k * (k + 1) // 2)

    barrier = pltpu.get_barrier_semaphore()

    copies = []
    for h in range(2):
        shift = jnp.where(core == h, 0, quarter)
        for b in range(quarter // LANES):
            source = pl.multiple_of(mate * half + shift + b * LANES, LANES)
            copies.append((
                inv.at[0, pl.ds(h * quarter, quarter), pl.ds(source, LANES)],
                packed.at[pl.ds(h * o_rows // 2 + b * quarter, quarter)],
            ))
    for k in range(blocks):
        source = pl.multiple_of(core * half + k * LANES, LANES)
        copies.append((
            inv.at[0, pl.ds(0, (k + 1) * LANES), pl.ds(source, LANES)],
            packed.at[pl.ds(base(k), (k + 1) * LANES)],
        ))
    copies = [pltpu.make_async_copy(s, d, pack_sem.at[i]) for i, (s, d) in enumerate(copies)]
    for c in copies:
        c.start()

    def greet(step, carry):
        pl.semaphore_signal(
            barrier, inc=1, device_id={"wide": lax.rem(me + step, n)}, device_id_type=MESH
        )
        return carry

    lax.fori_loop(1, n, greet, 0)
    pl.semaphore_signal(barrier, inc=1, device_id={"grad": mate}, device_id_type=MESH)
    pl.semaphore_wait(barrier, n)

    for c in copies:
        c.wait()

    for q in range(CHUNKS):
        def scatter(step, carry, q=q):
            peer = lax.rem(me + step, n)
            pltpu.make_async_remote_copy(
                src_ref=packed.at[pl.ds(pl.multiple_of((q * n + peer) * part, 16), part)],
                dst_ref=arrived[q].at[me],
                send_sem=send1.at[q],
                recv_sem=recv1.at[q],
                device_id={"wide": peer},
                device_id_type=MESH,
            ).start()
            return carry

        lax.fori_loop(1, n, scatter, 0)
        pltpu.make_async_copy(
            packed.at[pl.ds(pl.multiple_of((q * n + me) * part, 16), part)],
            arrived[q].at[me],
            recv1.at[q],
        ).start()

    def to_mate(src, dst, ssem, rsem):
        return pltpu.make_async_remote_copy(
            src_ref=src, dst_ref=dst, send_sem=ssem, recv_sem=rsem,
            device_id={"grad": mate}, device_id_type=MESH,
        )

    mine = pl.ds(pl.multiple_of(core * half, half), half)
    own_cols = pl.ds(pl.multiple_of(core * half, half), half)
    mate_cols = pl.ds(pl.multiple_of(mate * half, half), half)
    loads = [
        pltpu.make_async_copy(act.at[0, :, own_cols], a_own.at[mine], load_sem.at[0]),
        pltpu.make_async_copy(act.at[0, :, mate_cols], a_oth.at[mine], load_sem.at[1]),
        pltpu.make_async_copy(grad.at[0], g_own, load_sem.at[2]),
    ]
    swaps = [
        to_mate(act.at[0, :, mate_cols], a_own.at[mine], send_a.at[0], recv_a.at[0]),
        to_mate(act.at[0, :, own_cols], a_oth.at[mine], send_a.at[1], recv_a.at[1]),
        to_mate(grad.at[0], g_oth, send_g, recv_g),
    ]
    for c in loads + swaps:
        c.start()
    for c in loads:
        c.wait()
    for c in swaps:
        c.wait()

    count = live[me]
    width = lhs_t.shape[0]
    scale = count.astype(jnp.float32)

    def factor_rows(i, carry):
        strip = pl.ds(pl.multiple_of(i * width, width), width)
        keep = lax.broadcasted_iota(jnp.int32, (2 * half, width), 0) < count
        tile = a_own[:, strip]
        lhs_t[...] = jnp.where(keep, tile, jnp.zeros_like(tile)).T

        def factor_cols(j, inner):
            span = pl.ds(pl.multiple_of(j * width, width), width)
            row = i * width + lax.broadcasted_iota(jnp.int32, (width, width), 0)
            col = j * width + lax.broadcasted_iota(jnp.int32, (width, width), 1)
            m_own[strip, span] = (
                dot(lhs_t[...], a_own[:, span]) / scale + jnp.where(row == col, DAMPING, 0.0)
            ).astype(jnp.bfloat16)
            m_oth[strip, span] = (dot(lhs_t[...], a_oth[:, span]) / scale).astype(jnp.bfloat16)
            return inner

        return lax.fori_loop(0, half // width, factor_cols, carry)

    lax.fori_loop(0, half // width, factor_rows, 0)

    for q in range(CHUNKS):
        pltpu.make_async_copy(arrived[q], arrived[q], recv1.at[q]).wait()

        def choose(t, carry, q=q):
            stage[q * n + t] = arrived[q][sources[t]]
            return carry

        lax.fori_loop(0, n, choose, 0)
        landing = pl.ds(pl.multiple_of((q * n + me) * part, 16), part)

        def deliver(step, carry, q=q, landing=landing):
            peer = lax.rem(me + step, n)
            pltpu.make_async_remote_copy(
                src_ref=stage.at[q * n + peer],
                dst_ref=moved.at[landing],
                send_sem=send2.at[q],
                recv_sem=recv2.at[q],
                device_id={"wide": peer},
                device_id_type=MESH,
            ).start()
            return carry

        lax.fori_loop(1, n, deliver, 0)
        pltpu.make_async_copy(stage.at[q * n + me], moved.at[landing], recv2.at[q]).start()

    def off_product(h, left, x):
        shift = pl.multiple_of(jnp.where(core == h, 0, quarter), quarter)
        return dot(left[h, :, :quarter], x[pl.ds(shift, quarter)]) + dot(
            left[h, :, quarter:], x[pl.ds(pl.multiple_of(quarter - shift, quarter), quarter)]
        )

    off = to_mate(moved.at[pl.ds(0, o_rows)], o_in, send_o, recv_o)
    off_at, next_block = None, 0
    for q in range(CHUNKS):
        chunk = moved.at[pl.ds(q * n * part, n * part)]
        pltpu.make_async_copy(chunk, chunk, recv2.at[q]).wait()
        end = (q + 1) * n * part
        if off_at is None and end >= o_rows:
            off_at = q
            off.start()
            for h in range(2):
                for b in range(quarter // LANES):
                    s_o[h, :, b * LANES : (b + 1) * LANES] = moved[
                        pl.ds(h * o_rows // 2 + b * quarter, quarter)
                    ]
            off.wait()
            for h in range(2):
                other = jnp.where(mate == h, 0, o_rows // 2)
                for b in range(quarter // LANES):
                    at = pl.multiple_of(other + b * quarter, quarter)
                    s_o[h, b * LANES : (b + 1) * LANES, quarter:] = o_in[pl.ds(at, quarter)].T
            for h in range(2):
                first[h * quarter : (h + 1) * quarter] = off_product(h, s_o, g_oth)
        while off_at is not None and next_block < blocks and base(next_block + 1) <= end:
            k = next_block
            lanes = slice(k * LANES, (k + 1) * LANES)
            s_d[0 : (k + 1) * LANES, lanes] = moved[pl.ds(base(k), (k + 1) * LANES)]
            if k:
                s_d[lanes, 0 : k * LANES] = moved[pl.ds(base(k), k * LANES)].T
            next_block += 1

    tiles = [slice(i, i + width) for i in range(0, half, width)]
    for rows in tiles:
        first[rows] = first[rows] + dot(s_d[rows], g_own[...])
        f_own[rows] = first[rows].astype(jnp.bfloat16)
    swap = to_mate(f_own, f_oth, send_f, recv_f)
    swap.start()
    for rows in tiles:
        acc[rows] = dot(m_own[rows], f_own[...])
    swap.wait()
    for rows in tiles:
        c_own[rows] = (acc[rows] + dot(m_oth[rows], f_oth[...])).astype(jnp.bfloat16)
    swap = to_mate(c_own, c_oth, send_c, recv_c)
    swap.start()
    for rows in tiles:
        acc[rows] = 2.0 * first[rows] - dot(s_d[rows], c_own[...])
    swap.wait()
    for h in range(2):
        rows = slice(h * quarter, (h + 1) * quarter)
        out[0, rows] = (acc[rows] - off_product(h, s_o, c_oth)).astype(jnp.bfloat16)

    for q in range(CHUNKS):
        sent = moved.at[pl.ds(0, (n - 1) * part)]
        pltpu.make_async_copy(sent, sent, send1.at[q]).wait()
        pltpu.make_async_copy(sent, sent, send2.at[q]).wait()


def per_device(activations, inverse, gradients, matching, live_rows):
    n = lax.axis_size("wide")
    half, order = inverse.shape[1:]
    cols = gradients.shape[2]
    places = jnp.arange(n, dtype=jnp.int32)
    sources = jnp.sum(jnp.where(matching[None, :] == places[:, None], places[None, :], 0), axis=1)
    quarter = half // 2
    blocks = half // LANES
    o_rows = 2 * quarter * (quarter // LANES)
    used = o_rows + LANES * (blocks * (blocks + 1) // 2)
    part = -(-used // (16 * n * CHUNKS)) * 16
    full = part * n * CHUNKS
    bf16, f32 = jnp.bfloat16, jnp.float32
    dma = pltpu.SemaphoreType.DMA
    vmem = pltpu.VMEM
    pack_count = 2 * (quarter // LANES) + blocks
    scratch = [
        vmem((full, LANES), bf16),
        vmem((CHUNKS * n, part, LANES), bf16),
        vmem((full, LANES), bf16),
        vmem((o_rows, LANES), bf16),
        vmem((order, half), bf16),
        vmem((order, half), bf16),
        vmem((256, order), bf16),
        vmem((half, half), bf16),
        vmem((half, half), bf16),
        vmem((half, half), bf16),
        vmem((2, quarter, half), bf16),
        vmem((half, cols), bf16),
        vmem((half, cols), bf16),
        vmem((half, cols), f32),
        vmem((half, cols), f32),
        vmem((half, cols), bf16),
        vmem((half, cols), bf16),
        vmem((half, cols), bf16),
        vmem((half, cols), bf16),
    ]
    scratch += [vmem((n, part, LANES), bf16) for _ in range(CHUNKS)]
    scratch += [dma((pack_count,)), dma((3,))]
    scratch += [dma((CHUNKS,)) for _ in range(4)]
    scratch += [dma((2,)), dma((2,))] + [dma(()) for _ in range(8)]
    smem = pl.BlockSpec(memory_space=pltpu.SMEM)
    hbm = pl.BlockSpec(memory_space=pl.ANY)
    return pl.pallas_call(
        functools.partial(kernel, n, half, cols, part),
        out_shape=jax.ShapeDtypeStruct(gradients.shape, bf16),
        in_specs=[smem, smem, hbm, hbm, hbm],
        out_specs=pl.BlockSpec(memory_space=pltpu.VMEM),
        scratch_shapes=scratch,
        cost_estimate=pl.CostEstimate(
            flops=2 * half * order * (order + 3 * cols),
            bytes_accessed=4 * half * order + 4 * half * cols,
            transcendentals=0,
        ),
        compiler_params=pltpu.CompilerParams(
            collective_id=0, has_side_effects=True, vmem_limit_bytes=56 * 1024 * 1024
        ),
    )(sources, live_rows, activations, inverse, gradients)


def solution(mesh):
    return jax.shard_map(
        per_device,
        mesh=mesh,
        in_specs=(
            P(("dom", "wide"), "grad", None),
            P(("dom", "wide"), "grad", None),
            P(("dom", "wide"), "grad", None),
            P("dom"),
            P("dom"),
        ),
        out_specs=P(("dom", "wide"), "grad", None),
        check_vma=False,
    )
```

```python
import functools

import jax
import jax.numpy as jnp
from jax import lax
from jax.experimental import pallas as pl
from jax.experimental.pallas import tpu as pltpu
from jax.sharding import PartitionSpec as P

DAMPING = 1.0
LANES = 128
CHUNKS = 4
MESH = pl.DeviceIdType.MESH


def dot(a, b):
    return jnp.dot(a, b, preferred_element_type=jnp.float32)


def kernel(
    n, half, cols, part,
    sources, live, act, inv, grad, out,
    packed, stage, moved, o_in, a_own, a_oth, lhs_t, m_own, m_oth,
    s_d, s_o, g_own, g_oth, first, acc, f_own, f_oth, c_own, c_oth,
    *rest,
):
    arrived = rest[:CHUNKS]
    (pack_sem, load_sem, send1, recv1, send2, recv2,
     send_a, recv_a, send_g, recv_g, send_o, recv_o, send_f, recv_f, send_c, recv_c) = rest[CHUNKS:]
    me = lax.axis_index("wide")
    core = lax.axis_index("grad")
    mate = 1 - core
    quarter = half // 2
    blocks = half // LANES
    o_rows = 2 * quarter * (quarter // LANES)

    def base(k):
        return o_rows + LANES * (k * (k + 1) // 2)

    barrier = pltpu.get_barrier_semaphore()

    copies = []
    for h in range(2):
        shift = jnp.where(core == h, 0, quarter)
        for b in range(quarter // LANES):
            source = pl.multiple_of(mate * half + shift + b * LANES, LANES)
            copies.append((
                inv.at[0, pl.ds(h * quarter, quarter), pl.ds(source, LANES)],
                packed.at[pl.ds(h * o_rows // 2 + b * quarter, quarter)],
            ))
    for k in range(blocks):
        source = pl.multiple_of(core * half + k * LANES, LANES)
        copies.append((
            inv.at[0, pl.ds(0, (k + 1) * LANES), pl.ds(source, LANES)],
            packed.at[pl.ds(base(k), (k + 1) * LANES)],
        ))
    copies = [pltpu.make_async_copy(s, d, pack_sem.at[i]) for i, (s, d) in enumerate(copies)]
    for c in copies:
        c.start()

    def greet(step, carry):
        pl.semaphore_signal(
            barrier, inc=1, device_id={"wide": lax.rem(me + step, n)}, device_id_type=MESH
        )
        return carry

    lax.fori_loop(1, n, greet, 0)
    pl.semaphore_signal(barrier, inc=1, device_id={"grad": mate}, device_id_type=MESH)
    pl.semaphore_wait(barrier, n)

    for c in copies:
        c.wait()

    for q in range(CHUNKS):
        def scatter(step, carry, q=q):
            peer = lax.rem(me + step, n)
            pltpu.make_async_remote_copy(
                src_ref=packed.at[pl.ds(pl.multiple_of((q * n + peer) * part, 16), part)],
                dst_ref=arrived[q].at[me],
                send_sem=send1.at[q],
                recv_sem=recv1.at[q],
                device_id={"wide": peer},
                device_id_type=MESH,
            ).start()
            return carry

        lax.fori_loop(1, n, scatter, 0)
        pltpu.make_async_copy(
            packed.at[pl.ds(pl.multiple_of((q * n + me) * part, 16), part)],
            arrived[q].at[me],
            recv1.at[q],
        ).start()

    def to_mate(src, dst, ssem, rsem):
        return pltpu.make_async_remote_copy(
            src_ref=src, dst_ref=dst, send_sem=ssem, recv_sem=rsem,
            device_id={"grad": mate}, device_id_type=MESH,
        )

    mine = pl.ds(pl.multiple_of(core * half, half), half)
    own_cols = pl.ds(pl.multiple_of(core * half, half), half)
    mate_cols = pl.ds(pl.multiple_of(mate * half, half), half)
    loads = [
        pltpu.make_async_copy(act.at[0, :, own_cols], a_own.at[mine], load_sem.at[0]),
        pltpu.make_async_copy(act.at[0, :, mate_cols], a_oth.at[mine], load_sem.at[1]),
        pltpu.make_async_copy(grad.at[0], g_own, load_sem.at[2]),
    ]
    swaps = [
        to_mate(act.at[0, :, mate_cols], a_own.at[mine], send_a.at[0], recv_a.at[0]),
        to_mate(act.at[0, :, own_cols], a_oth.at[mine], send_a.at[1], recv_a.at[1]),
        to_mate(grad.at[0], g_oth, send_g, recv_g),
    ]
    for c in loads + swaps:
        c.start()
    for c in loads:
        c.wait()
    for c in swaps:
        c.wait()

    count = live[me]
    width = lhs_t.shape[0]
    scale = count.astype(jnp.float32)

    def factor_rows(i, carry):
        strip = pl.ds(pl.multiple_of(i * width, width), width)
        keep = lax.broadcasted_iota(jnp.int32, (2 * half, width), 0) < count
        tile = a_own[:, strip]
        lhs_t[...] = jnp.where(keep, tile, jnp.zeros_like(tile)).T

        def factor_cols(j, inner):
            span = pl.ds(pl.multiple_of(j * width, width), width)
            row = i * width + lax.broadcasted_iota(jnp.int32, (width, width), 0)
            col = j * width + lax.broadcasted_iota(jnp.int32, (width, width), 1)
            m_own[strip, span] = (
                dot(lhs_t[...], a_own[:, span]) / scale + jnp.where(row == col, DAMPING, 0.0)
            ).astype(jnp.bfloat16)
            m_oth[strip, span] = (dot(lhs_t[...], a_oth[:, span]) / scale).astype(jnp.bfloat16)
            return inner

        return lax.fori_loop(0, half // width, factor_cols, carry)

    lax.fori_loop(0, half // width, factor_rows, 0)

    for q in range(CHUNKS):
        pltpu.make_async_copy(arrived[q], arrived[q], recv1.at[q]).wait()

        def choose(t, carry, q=q):
            stage[q * n + t] = arrived[q][sources[t]]
            return carry

        lax.fori_loop(0, n, choose, 0)
        landing = pl.ds(pl.multiple_of((q * n + me) * part, 16), part)

        def deliver(step, carry, q=q, landing=landing):
            peer = lax.rem(me + step, n)
            pltpu.make_async_remote_copy(
                src_ref=stage.at[q * n + peer],
                dst_ref=moved.at[landing],
                send_sem=send2.at[q],
                recv_sem=recv2.at[q],
                device_id={"wide": peer},
                device_id_type=MESH,
            ).start()
            return carry

        lax.fori_loop(1, n, deliver, 0)
        pltpu.make_async_copy(stage.at[q * n + me], moved.at[landing], recv2.at[q]).start()

    def off_product(h, left, x):
        shift = pl.multiple_of(jnp.where(core == h, 0, quarter), quarter)
        return dot(left[h, :, :quarter], x[pl.ds(shift, quarter)]) + dot(
            left[h, :, quarter:], x[pl.ds(pl.multiple_of(quarter - shift, quarter), quarter)]
        )

    off = to_mate(moved.at[pl.ds(0, o_rows)], o_in, send_o, recv_o)
    off_at, next_block = None, 0
    for q in range(CHUNKS):
        chunk = moved.at[pl.ds(q * n * part, n * part)]
        pltpu.make_async_copy(chunk, chunk, recv2.at[q]).wait()
        end = (q + 1) * n * part
        if off_at is None and end >= o_rows:
            off_at = q
            off.start()
            for h in range(2):
                for b in range(quarter // LANES):
                    s_o[h, :, b * LANES : (b + 1) * LANES] = moved[
                        pl.ds(h * o_rows // 2 + b * quarter, quarter)
                    ]
            off.wait()
            for h in range(2):
                other = jnp.where(mate == h, 0, o_rows // 2)
                for b in range(quarter // LANES):
                    at = pl.multiple_of(other + b * quarter, quarter)
                    s_o[h, b * LANES : (b + 1) * LANES, quarter:] = o_in[pl.ds(at, quarter)].T
            for h in range(2):
                first[h * quarter : (h + 1) * quarter] = off_product(h, s_o, g_oth)
        while off_at is not None and next_block < blocks and base(next_block + 1) <= end:
            k = next_block
            lanes = slice(k * LANES, (k + 1) * LANES)
            s_d[0 : (k + 1) * LANES, lanes] = moved[pl.ds(base(k), (k + 1) * LANES)]
            if k:
                s_d[lanes, 0 : k * LANES] = moved[pl.ds(base(k), k * LANES)].T
            next_block += 1

    tiles = [slice(i, i + width) for i in range(0, half, width)]
    for rows in tiles:
        first[rows] = first[rows] + dot(s_d[rows], g_own[...])
        f_own[rows] = first[rows].astype(jnp.bfloat16)
    swap = to_mate(f_own, f_oth, send_f, recv_f)
    swap.start()
    for rows in tiles:
        acc[rows] = dot(m_own[rows], f_own[...])
    swap.wait()
    for rows in tiles:
        c_own[rows] = (acc[rows] + dot(m_oth[rows], f_oth[...])).astype(jnp.bfloat16)
    swap = to_mate(c_own, c_oth, send_c, recv_c)
    swap.start()
    for rows in tiles:
        acc[rows] = 2.0 * first[rows] - dot(s_d[rows], c_own[...])
    swap.wait()
    for h in range(2):
        rows = slice(h * quarter, (h + 1) * quarter)
        out[0, rows] = (acc[rows] - off_product(h, s_o, c_oth)).astype(jnp.bfloat16)

    for q in range(CHUNKS):
        sent = moved.at[pl.ds(0, (n - 1) * part)]
        pltpu.make_async_copy(sent, sent, send1.at[q]).wait()
        pltpu.make_async_copy(sent, sent, send2.at[q]).wait()


STEPS = 8


def line_kernel(
    n, half, cols, part, many,
    route, live, act, inv, grad, out,
    packed, stage_b, stage_c, moved, o_in, a_own, a_oth, lhs_t, m_own, m_oth,
    s_d, s_o, g_own, g_oth, first, acc, f_own, f_oth, c_own, c_oth,
    *rest,
):
    near, far, relay = rest[:STEPS], rest[STEPS : 2 * STEPS], rest[2 * STEPS : 3 * STEPS]
    (pack_sem, load_sem, send1, recv1, send2, recv2, send3, recv3, send4, recv4,
     send_a, recv_a, send_g, recv_g, send_o, recv_o, send_f, recv_f, send_c, recv_c) = rest[3 * STEPS:]
    me = lax.axis_index("wide")
    core = lax.axis_index("grad")
    mate = 1 - core
    side, local, rail = me // 4, lax.rem(me, 4), lax.rem(me, 2)
    inner = local // 2 == 1 - side
    outer = local // 2 == side
    inner_at, outer_at = 2 * (1 - side), 2 * side
    across = 2 * (2 - side) + rail
    quarter = half // 2
    blocks = half // LANES
    o_rows = 2 * quarter * (quarter // LANES)

    def base(k):
        return o_rows + LANES * (k * (k + 1) // 2)

    def slot(ref, q, r):
        return ref.at[pl.ds(pl.multiple_of((2 * q + r) * part, 16), part)]

    def to_wide(src, dst, ssem, rsem, peer):
        return pltpu.make_async_remote_copy(
            src_ref=src, dst_ref=dst, send_sem=ssem, recv_sem=rsem,
            device_id={"wide": peer}, device_id_type=MESH,
        )

    barrier = pltpu.get_barrier_semaphore()

    copies = []
    for h in range(2):
        shift = jnp.where(core == h, 0, quarter)
        for b in range(quarter // LANES):
            source = pl.multiple_of(mate * half + shift + b * LANES, LANES)
            copies.append((
                inv.at[0, pl.ds(h * quarter, quarter), pl.ds(source, LANES)],
                packed.at[pl.ds(h * o_rows // 2 + b * quarter, quarter)],
            ))
    for k in range(blocks):
        source = pl.multiple_of(core * half + k * LANES, LANES)
        copies.append((
            inv.at[0, pl.ds(0, (k + 1) * LANES), pl.ds(source, LANES)],
            packed.at[pl.ds(base(k), (k + 1) * LANES)],
        ))
    copies = [pltpu.make_async_copy(s, d, pack_sem.at[i]) for i, (s, d) in enumerate(copies)]
    for c in copies:
        c.start()

    def greet(step, carry):
        pl.semaphore_signal(
            barrier, inc=1, device_id={"wide": lax.rem(me + step, n)}, device_id_type=MESH
        )
        return carry

    lax.fori_loop(1, n, greet, 0)
    pl.semaphore_signal(barrier, inc=1, device_id={"grad": mate}, device_id_type=MESH)
    pl.semaphore_wait(barrier, n)

    for c in copies:
        c.wait()

    @pl.when(outer)
    def _():
        for q in range(STEPS):
            for r in range(2):
                to_wide(
                    slot(packed, q, r), near[q].at[local], send1.at[q], recv1.at[q],
                    4 * side + inner_at + r,
                ).start()

    @pl.when(inner)
    def _():
        for q in range(STEPS):
            to_wide(
                slot(packed, q, 1 - rail), near[q].at[local], send1.at[q], recv1.at[q],
                4 * side + inner_at + 1 - rail,
            ).start()
            pltpu.make_async_copy(slot(packed, q, rail), near[q].at[local], recv1.at[q]).start()

    def to_mate(src, dst, ssem, rsem):
        return pltpu.make_async_remote_copy(
            src_ref=src, dst_ref=dst, send_sem=ssem, recv_sem=rsem,
            device_id={"grad": mate}, device_id_type=MESH,
        )

    mine = pl.ds(pl.multiple_of(core * half, half), half)
    own_cols = pl.ds(pl.multiple_of(core * half, half), half)
    mate_cols = pl.ds(pl.multiple_of(mate * half, half), half)
    loads = [
        pltpu.make_async_copy(act.at[0, :, own_cols], a_own.at[mine], load_sem.at[0]),
        pltpu.make_async_copy(act.at[0, :, mate_cols], a_oth.at[mine], load_sem.at[1]),
        pltpu.make_async_copy(grad.at[0], g_own, load_sem.at[2]),
    ]
    swaps = [
        to_mate(act.at[0, :, mate_cols], a_own.at[mine], send_a.at[0], recv_a.at[0]),
        to_mate(act.at[0, :, own_cols], a_oth.at[mine], send_a.at[1], recv_a.at[1]),
        to_mate(grad.at[0], g_oth, send_g, recv_g),
    ]
    for c in loads + swaps:
        c.start()
    count = live[me]
    width = lhs_t.shape[0]
    scale = count.astype(jnp.float32)

    def factor_rows(i, carry):
        strip = pl.ds(pl.multiple_of(i * width, width), width)
        keep = lax.broadcasted_iota(jnp.int32, (2 * half, width), 0) < count
        tile = a_own[:, strip]
        lhs_t[...] = jnp.where(keep, tile, jnp.zeros_like(tile)).T

        def factor_cols(j, inner):
            span = pl.ds(pl.multiple_of(j * width, width), width)
            row = i * width + lax.broadcasted_iota(jnp.int32, (width, width), 0)
            col = j * width + lax.broadcasted_iota(jnp.int32, (width, width), 1)
            m_own[strip, span] = (
                dot(lhs_t[...], a_own[:, span]) / scale + jnp.where(row == col, DAMPING, 0.0)
            ).astype(jnp.bfloat16)
            m_oth[strip, span] = (dot(lhs_t[...], a_oth[:, span]) / scale).astype(jnp.bfloat16)
            return inner

        return lax.fori_loop(0, half // width, factor_cols, carry)

    def off_product(h, left, x):
        shift = pl.multiple_of(jnp.where(core == h, 0, quarter), quarter)
        return dot(left[h, :, :quarter], x[pl.ds(shift, quarter)]) + dot(
            left[h, :, quarter:], x[pl.ds(pl.multiple_of(quarter - shift, quarter), quarter)]
        )

    def cross(q):
        pltpu.make_async_copy(near[q], near[q], recv1.at[q]).wait()
        for i in range(many):
            stage_b[q * many + i] = near[q][route[4 * side + i]]
        to_wide(
            stage_b.at[pl.ds(q * many, many)], far[q], send2.at[q], recv2.at[q], across
        ).start()

    def deliver(q):
        pltpu.make_async_copy(far[q], far[q], recv2.at[q]).wait()
        for i in range(4):
            t = 4 * side + i
            crossed = jnp.full((part, LANES), route[8 + t], jnp.int32) != 0
            stage_c[4 * q + i] = jnp.where(
                crossed, far[q][route[24 + t]], near[q][route[16 + t]]
            )
        pltpu.make_async_copy(
            stage_c.at[4 * q + inner_at + rail], slot(moved, q, rail), recv3.at[q]
        ).start()
        to_wide(
            stage_c.at[4 * q + inner_at + 1 - rail], slot(moved, q, rail), send3.at[q], recv3.at[q],
            4 * side + inner_at + 1 - rail,
        ).start()
        to_wide(
            stage_c.at[4 * q + outer_at + 1 - rail], relay[q], send3.at[q], recv4.at[q],
            4 * side + outer_at + rail,
        ).start()
        to_wide(
            stage_c.at[4 * q + outer_at + rail], slot(moved, q, rail), send3.at[q], recv3.at[q],
            4 * side + outer_at + rail,
        ).start()

    def pass_on(q):
        pltpu.make_async_copy(relay[q], relay[q], recv4.at[q]).wait()
        to_wide(
            relay[q], slot(moved, q, rail), send4.at[q], recv3.at[q],
            4 * side + outer_at + 1 - rail,
        ).start()

    off = to_mate(moved.at[pl.ds(0, o_rows)], o_in, send_o, recv_o)
    off_at = -(-o_rows // (2 * part)) - 1

    def finish_off():
        off.wait()
        for h in range(2):
            other = jnp.where(mate == h, 0, o_rows // 2)
            for b in range(quarter // LANES):
                at = pl.multiple_of(other + b * quarter, quarter)
                s_o[h, b * LANES : (b + 1) * LANES, quarter:] = o_in[pl.ds(at, quarter)].T
        for h in range(2):
            first[h * quarter : (h + 1) * quarter] = off_product(h, s_o, g_oth)

    def assemble(q, next_block):
        chunk = moved.at[pl.ds(2 * q * part, 2 * part)]
        pltpu.make_async_copy(chunk, chunk, recv3.at[q]).wait()
        if q == off_at:
            off.start()
            for h in range(2):
                for b in range(quarter // LANES):
                    s_o[h, :, b * LANES : (b + 1) * LANES] = moved[
                        pl.ds(h * o_rows // 2 + b * quarter, quarter)
                    ]
        if q == min(off_at + 1, STEPS - 1):
            finish_off()
        while next_block < blocks and base(next_block + 1) <= 2 * (q + 1) * part:
            k = next_block
            lanes = slice(k * LANES, (k + 1) * LANES)
            s_d[0 : (k + 1) * LANES, lanes] = moved[pl.ds(base(k), (k + 1) * LANES)]
            if k:
                s_d[lanes, 0 : k * LANES] = moved[pl.ds(base(k), k * LANES)].T
            next_block += 1
        return next_block

    next_block, strips = 0, half // width
    for step in range(max(STEPS + 2, strips + 1)):
        if step < STEPS:
            pl.when(inner)(functools.partial(cross, step))
        if 1 <= step <= STEPS:
            pl.when(inner)(functools.partial(deliver, step - 1))
            pl.when(outer)(functools.partial(pass_on, step - 1))
        if step == 1:
            for c in loads + swaps:
                c.wait()
        if 1 <= step <= strips:
            factor_rows(step - 1, 0)
        if 2 <= step < STEPS + 2:
            next_block = assemble(step - 2, next_block)

    tiles = [slice(i, i + width) for i in range(0, half, width)]
    for rows in tiles:
        first[rows] = first[rows] + dot(s_d[rows], g_own[...])
        f_own[rows] = first[rows].astype(jnp.bfloat16)
    swap = to_mate(f_own, f_oth, send_f, recv_f)
    swap.start()
    for rows in tiles:
        acc[rows] = dot(m_own[rows], f_own[...])
    swap.wait()
    for rows in tiles:
        c_own[rows] = (acc[rows] + dot(m_oth[rows], f_oth[...])).astype(jnp.bfloat16)
    swap = to_mate(c_own, c_oth, send_c, recv_c)
    swap.start()
    for rows in tiles:
        acc[rows] = 2.0 * first[rows] - dot(s_d[rows], c_own[...])
    swap.wait()
    for h in range(2):
        rows = slice(h * quarter, (h + 1) * quarter)
        out[0, rows] = (acc[rows] - off_product(h, s_o, c_oth)).astype(jnp.bfloat16)

    def sent(sems, count):
        rows = moved.at[pl.ds(0, count * part)]
        for q in range(STEPS):
            pltpu.make_async_copy(rows, rows, sems.at[q]).wait()

    @pl.when(outer)
    def _():
        sent(send1, 2)
        sent(send4, 1)

    @pl.when(inner)
    def _():
        sent(send1, 1)
        sent(send2, many)
        sent(send3, 3)


def run(n, many, operands):
    table, live_rows, activations, inverse, gradients = operands
    half, order = inverse.shape[1:]
    cols = gradients.shape[2]
    quarter = half // 2
    blocks = half // LANES
    o_rows = 2 * quarter * (quarter // LANES)
    used = o_rows + LANES * (blocks * (blocks + 1) // 2)
    pieces = n * CHUNKS if many is None else 2 * STEPS
    part = -(-used // (16 * pieces)) * 16
    full = part * pieces
    bf16, f32 = jnp.bfloat16, jnp.float32
    dma = pltpu.SemaphoreType.DMA
    vmem = pltpu.VMEM
    pack_count = 2 * (quarter // LANES) + blocks
    if many is None:
        stages = [vmem((pieces, part, LANES), bf16)]
    else:
        stages = [vmem((k * STEPS, part, LANES), bf16) for k in (many, 4)]
    scratch = [
        vmem((full, LANES), bf16),
        *stages,
        vmem((full, LANES), bf16),
        vmem((o_rows, LANES), bf16),
        vmem((order, half), bf16),
        vmem((order, half), bf16),
        vmem((256, order), bf16),
        vmem((half, half), bf16),
        vmem((half, half), bf16),
        vmem((half, half), bf16),
        vmem((2, quarter, half), bf16),
        vmem((half, cols), bf16),
        vmem((half, cols), bf16),
        vmem((half, cols), f32),
        vmem((half, cols), f32),
        vmem((half, cols), bf16),
        vmem((half, cols), bf16),
        vmem((half, cols), bf16),
        vmem((half, cols), bf16),
    ]
    if many is None:
        body = functools.partial(kernel, n, half, cols, part)
        scratch += [vmem((n, part, LANES), bf16) for _ in range(CHUNKS)]
        chunk_sems = [dma((CHUNKS,)) for _ in range(4)]
    else:
        body = functools.partial(line_kernel, n, half, cols, part, many)
        scratch += [vmem((4, part, LANES), bf16) for _ in range(STEPS)]
        scratch += [vmem((many, part, LANES), bf16) for _ in range(STEPS)]
        scratch += [vmem((part, LANES), bf16) for _ in range(STEPS)]
        chunk_sems = [dma((STEPS,)) for _ in range(8)]
    scratch += [dma((pack_count,)), dma((3,))]
    scratch += chunk_sems
    scratch += [dma((2,)), dma((2,))] + [dma(()) for _ in range(8)]
    smem = pl.BlockSpec(memory_space=pltpu.SMEM)
    hbm = pl.BlockSpec(memory_space=pl.ANY)
    return pl.pallas_call(
        body,
        out_shape=jax.ShapeDtypeStruct(gradients.shape, bf16),
        in_specs=[smem, smem, hbm, hbm, hbm],
        out_specs=pl.BlockSpec(memory_space=pltpu.VMEM),
        scratch_shapes=scratch,
        cost_estimate=pl.CostEstimate(
            flops=2 * half * order * (order + 3 * cols),
            bytes_accessed=4 * half * order + 4 * half * cols,
            transcendentals=0,
        ),
        compiler_params=pltpu.CompilerParams(
            collective_id=many or 0, has_side_effects=True, vmem_limit_bytes=56 * 1024 * 1024
        ),
    )(table, live_rows, activations, inverse, gradients)


def per_device(activations, inverse, gradients, matching, live_rows):
    n = lax.axis_size("wide")
    places = jnp.arange(n, dtype=jnp.int32)
    sources = jnp.sum(jnp.where(matching[None, :] == places[:, None], places[None, :], 0), axis=1)
    if n != 8:
        return run(n, None, (sources, live_rows, activations, inverse, gradients))
    side = places // 4
    cross = matching // 4 != side
    earlier = (side[None, :] == side[:, None]) & (places[None, :] < places[:, None])
    rank = jnp.sum(jnp.where(earlier & cross[None, :], 1, 0), axis=1)
    wanted = (side[None, :] == side[:, None]) & cross[None, :] & (
        rank[None, :] == (places % 4)[:, None]
    )
    leaving = jnp.sum(jnp.where(wanted, (places % 4)[None, :], 0), axis=1)
    comes = sources // 4 != side
    from_rank = jnp.sum(
        jnp.where((matching[None, :] == places[:, None]) & cross[None, :], rank[None, :], 0), axis=1
    )
    route = jnp.concatenate([leaving, comes.astype(jnp.int32), sources % 4, from_rank])
    many = jnp.sum(jnp.where(cross & (side == 0), 1, 0)).reshape(1)
    doms = lax.axis_size("dom")
    most, passed = many, many
    for _ in range(doms - 1):
        passed = lax.ppermute(passed, "dom", [(d, (d + 1) % doms) for d in range(doms)])
        most = jnp.maximum(most, passed)
    return lax.switch(
        jnp.clip(most[0] - 2, 0, 2),
        [functools.partial(run, n, k) for k in (2, 3, 4)],
        (route.astype(jnp.int32), live_rows, activations, inverse, gradients),
    )


def solution(mesh):
    return jax.shard_map(
        per_device,
        mesh=mesh,
        in_specs=(
            P(("dom", "wide"), "grad", None),
            P(("dom", "wide"), "grad", None),
            P(("dom", "wide"), "grad", None),
            P("dom"),
            P("dom"),
        ),
        out_specs=P(("dom", "wide"), "grad", None),
        check_vma=False,
    )
```

```python
import functools

import jax
import jax.numpy as jnp
from jax import lax
from jax.experimental import pallas as pl
from jax.experimental.pallas import tpu as pltpu
from jax.sharding import PartitionSpec as P

DAMPING = 1.0
LANES = 128
CHUNKS = 4
MESH = pl.DeviceIdType.MESH


def dot(a, b):
    return jnp.dot(a, b, preferred_element_type=jnp.float32)


def kernel(
    n, half, cols, part,
    sources, live, act, inv, grad, out,
    packed, stage, moved, o_in, a_own, a_oth, lhs_t, m_own, m_oth,
    s_d, s_o, g_own, g_oth, first, acc, f_own, f_oth, c_own, c_oth,
    *rest,
):
    arrived = rest[:CHUNKS]
    (pack_sem, load_sem, send1, recv1, send2, recv2,
     send_a, recv_a, send_g, recv_g, send_o, recv_o, send_f, recv_f, send_c, recv_c) = rest[CHUNKS:]
    me = lax.axis_index("wide")
    core = lax.axis_index("grad")
    mate = 1 - core
    quarter = half // 2
    blocks = half // LANES
    o_rows = 2 * quarter * (quarter // LANES)

    def base(k):
        return o_rows + LANES * (k * (k + 1) // 2)

    barrier = pltpu.get_barrier_semaphore()

    copies = []
    for h in range(2):
        shift = jnp.where(core == h, 0, quarter)
        for b in range(quarter // LANES):
            source = pl.multiple_of(mate * half + shift + b * LANES, LANES)
            copies.append((
                inv.at[0, pl.ds(h * quarter, quarter), pl.ds(source, LANES)],
                packed.at[pl.ds(h * o_rows // 2 + b * quarter, quarter)],
            ))
    for k in range(blocks):
        source = pl.multiple_of(core * half + k * LANES, LANES)
        copies.append((
            inv.at[0, pl.ds(0, (k + 1) * LANES), pl.ds(source, LANES)],
            packed.at[pl.ds(base(k), (k + 1) * LANES)],
        ))
    copies = [pltpu.make_async_copy(s, d, pack_sem.at[i]) for i, (s, d) in enumerate(copies)]
    for c in copies:
        c.start()

    def greet(step, carry):
        pl.semaphore_signal(
            barrier, inc=1, device_id={"wide": lax.rem(me + step, n)}, device_id_type=MESH
        )
        return carry

    lax.fori_loop(1, n, greet, 0)
    pl.semaphore_signal(barrier, inc=1, device_id={"grad": mate}, device_id_type=MESH)
    pl.semaphore_wait(barrier, n)

    for c in copies:
        c.wait()

    for q in range(CHUNKS):
        def scatter(step, carry, q=q):
            peer = lax.rem(me + step, n)
            pltpu.make_async_remote_copy(
                src_ref=packed.at[pl.ds(pl.multiple_of((q * n + peer) * part, 16), part)],
                dst_ref=arrived[q].at[me],
                send_sem=send1.at[q],
                recv_sem=recv1.at[q],
                device_id={"wide": peer},
                device_id_type=MESH,
            ).start()
            return carry

        lax.fori_loop(1, n, scatter, 0)
        pltpu.make_async_copy(
            packed.at[pl.ds(pl.multiple_of((q * n + me) * part, 16), part)],
            arrived[q].at[me],
            recv1.at[q],
        ).start()

    def to_mate(src, dst, ssem, rsem):
        return pltpu.make_async_remote_copy(
            src_ref=src, dst_ref=dst, send_sem=ssem, recv_sem=rsem,
            device_id={"grad": mate}, device_id_type=MESH,
        )

    mine = pl.ds(pl.multiple_of(core * half, half), half)
    own_cols = pl.ds(pl.multiple_of(core * half, half), half)
    mate_cols = pl.ds(pl.multiple_of(mate * half, half), half)
    loads = [
        pltpu.make_async_copy(act.at[0, :, own_cols], a_own.at[mine], load_sem.at[0]),
        pltpu.make_async_copy(act.at[0, :, mate_cols], a_oth.at[mine], load_sem.at[1]),
        pltpu.make_async_copy(grad.at[0], g_own, load_sem.at[2]),
    ]
    swaps = [
        to_mate(act.at[0, :, mate_cols], a_own.at[mine], send_a.at[0], recv_a.at[0]),
        to_mate(act.at[0, :, own_cols], a_oth.at[mine], send_a.at[1], recv_a.at[1]),
        to_mate(grad.at[0], g_oth, send_g, recv_g),
    ]
    for c in loads + swaps:
        c.start()
    for c in loads:
        c.wait()
    for c in swaps:
        c.wait()

    count = live[me]
    width = lhs_t.shape[0]
    scale = count.astype(jnp.float32)

    def factor_rows(i, carry):
        strip = pl.ds(pl.multiple_of(i * width, width), width)
        keep = lax.broadcasted_iota(jnp.int32, (2 * half, width), 0) < count
        tile = a_own[:, strip]
        lhs_t[...] = jnp.where(keep, tile, jnp.zeros_like(tile)).T

        def factor_cols(j, inner):
            span = pl.ds(pl.multiple_of(j * width, width), width)
            row = i * width + lax.broadcasted_iota(jnp.int32, (width, width), 0)
            col = j * width + lax.broadcasted_iota(jnp.int32, (width, width), 1)
            m_own[strip, span] = (
                dot(lhs_t[...], a_own[:, span]) / scale + jnp.where(row == col, DAMPING, 0.0)
            ).astype(jnp.bfloat16)
            m_oth[strip, span] = (dot(lhs_t[...], a_oth[:, span]) / scale).astype(jnp.bfloat16)
            return inner

        return lax.fori_loop(0, half // width, factor_cols, carry)

    lax.fori_loop(0, half // width, factor_rows, 0)

    for q in range(CHUNKS):
        pltpu.make_async_copy(arrived[q], arrived[q], recv1.at[q]).wait()

        def choose(t, carry, q=q):
            stage[q * n + t] = arrived[q][sources[t]]
            return carry

        lax.fori_loop(0, n, choose, 0)
        landing = pl.ds(pl.multiple_of((q * n + me) * part, 16), part)

        def deliver(step, carry, q=q, landing=landing):
            peer = lax.rem(me + step, n)
            pltpu.make_async_remote_copy(
                src_ref=stage.at[q * n + peer],
                dst_ref=moved.at[landing],
                send_sem=send2.at[q],
                recv_sem=recv2.at[q],
                device_id={"wide": peer},
                device_id_type=MESH,
            ).start()
            return carry

        lax.fori_loop(1, n, deliver, 0)
        pltpu.make_async_copy(stage.at[q * n + me], moved.at[landing], recv2.at[q]).start()

    def off_product(h, left, x):
        shift = pl.multiple_of(jnp.where(core == h, 0, quarter), quarter)
        return dot(left[h, :, :quarter], x[pl.ds(shift, quarter)]) + dot(
            left[h, :, quarter:], x[pl.ds(pl.multiple_of(quarter - shift, quarter), quarter)]
        )

    off = to_mate(moved.at[pl.ds(0, o_rows)], o_in, send_o, recv_o)
    off_at, next_block = None, 0
    for q in range(CHUNKS):
        chunk = moved.at[pl.ds(q * n * part, n * part)]
        pltpu.make_async_copy(chunk, chunk, recv2.at[q]).wait()
        end = (q + 1) * n * part
        if off_at is None and end >= o_rows:
            off_at = q
            off.start()
            for h in range(2):
                for b in range(quarter // LANES):
                    s_o[h, :, b * LANES : (b + 1) * LANES] = moved[
                        pl.ds(h * o_rows // 2 + b * quarter, quarter)
                    ]
            off.wait()
            for h in range(2):
                other = jnp.where(mate == h, 0, o_rows // 2)
                for b in range(quarter // LANES):
                    at = pl.multiple_of(other + b * quarter, quarter)
                    s_o[h, b * LANES : (b + 1) * LANES, quarter:] = o_in[pl.ds(at, quarter)].T
            for h in range(2):
                first[h * quarter : (h + 1) * quarter] = off_product(h, s_o, g_oth)
        while off_at is not None and next_block < blocks and base(next_block + 1) <= end:
            k = next_block
            lanes = slice(k * LANES, (k + 1) * LANES)
            s_d[0 : (k + 1) * LANES, lanes] = moved[pl.ds(base(k), (k + 1) * LANES)]
            if k:
                s_d[lanes, 0 : k * LANES] = moved[pl.ds(base(k), k * LANES)].T
            next_block += 1

    tiles = [slice(i, i + width) for i in range(0, half, width)]
    for rows in tiles:
        first[rows] = first[rows] + dot(s_d[rows], g_own[...])
        f_own[rows] = first[rows].astype(jnp.bfloat16)
    swap = to_mate(f_own, f_oth, send_f, recv_f)
    swap.start()
    for rows in tiles:
        acc[rows] = dot(m_own[rows], f_own[...])
    swap.wait()
    for rows in tiles:
        c_own[rows] = (acc[rows] + dot(m_oth[rows], f_oth[...])).astype(jnp.bfloat16)
    swap = to_mate(c_own, c_oth, send_c, recv_c)
    swap.start()
    for rows in tiles:
        acc[rows] = 2.0 * first[rows] - dot(s_d[rows], c_own[...])
    swap.wait()
    for h in range(2):
        rows = slice(h * quarter, (h + 1) * quarter)
        out[0, rows] = (acc[rows] - off_product(h, s_o, c_oth)).astype(jnp.bfloat16)

    for q in range(CHUNKS):
        sent = moved.at[pl.ds(0, (n - 1) * part)]
        pltpu.make_async_copy(sent, sent, send1.at[q]).wait()
        pltpu.make_async_copy(sent, sent, send2.at[q]).wait()


STEPS = 16
WINDOW = 2
LAG = 3


def line_kernel(
    n, half, cols, part, many,
    route, live, act, inv, grad, out,
    packed, stage_b, stage_c, moved, o_in, a_own, a_oth, lhs_t, m_own, m_oth,
    s_d, s_o, g_own, g_oth, first, acc, f_own, f_oth, c_own, c_oth,
    *rest,
):
    near, far, relay = rest[:STEPS], rest[STEPS : 2 * STEPS], rest[2 * STEPS : 3 * STEPS]
    (pack_sem, load_sem, send1, recv1, send2, recv2, send3, recv3, send4, recv4,
     send_a, recv_a, send_g, recv_g, send_o, recv_o, send_f, recv_f, send_c, recv_c) = rest[3 * STEPS:]
    me = lax.axis_index("wide")
    core = lax.axis_index("grad")
    mate = 1 - core
    side, local, rail = me // 4, lax.rem(me, 4), lax.rem(me, 2)
    inner = local // 2 == 1 - side
    outer = local // 2 == side
    inner_at, outer_at = 2 * (1 - side), 2 * side
    across = 2 * (2 - side) + rail
    quarter = half // 2
    blocks = half // LANES
    o_rows = 2 * quarter * (quarter // LANES)

    def base(k):
        return o_rows + LANES * (k * (k + 1) // 2)

    def slot(ref, q, r):
        return ref.at[pl.ds(pl.multiple_of((2 * q + r) * part, 16), part)]

    def to_wide(src, dst, ssem, rsem, peer):
        return pltpu.make_async_remote_copy(
            src_ref=src, dst_ref=dst, send_sem=ssem, recv_sem=rsem,
            device_id={"wide": peer}, device_id_type=MESH,
        )

    barrier = pltpu.get_barrier_semaphore()

    copies = []
    for h in range(2):
        shift = jnp.where(core == h, 0, quarter)
        for b in range(quarter // LANES):
            source = pl.multiple_of(mate * half + shift + b * LANES, LANES)
            copies.append((
                inv.at[0, pl.ds(h * quarter, quarter), pl.ds(source, LANES)],
                packed.at[pl.ds(h * o_rows // 2 + b * quarter, quarter)],
            ))
    for k in range(blocks):
        source = pl.multiple_of(core * half + k * LANES, LANES)
        copies.append((
            inv.at[0, pl.ds(0, (k + 1) * LANES), pl.ds(source, LANES)],
            packed.at[pl.ds(base(k), (k + 1) * LANES)],
        ))
    copies = [pltpu.make_async_copy(s, d, pack_sem.at[i]) for i, (s, d) in enumerate(copies)]
    for c in copies:
        c.start()

    def greet(step, carry):
        pl.semaphore_signal(
            barrier, inc=1, device_id={"wide": lax.rem(me + step, n)}, device_id_type=MESH
        )
        return carry

    lax.fori_loop(1, n, greet, 0)
    pl.semaphore_signal(barrier, inc=1, device_id={"grad": mate}, device_id_type=MESH)
    pl.semaphore_wait(barrier, n)

    for c in copies:
        c.wait()

    def start_outer(q):
        for r in range(2):
            to_wide(
                slot(packed, q, r), near[q].at[local], send1.at[q], recv1.at[q],
                4 * side + inner_at + r,
            ).start()

    def start_inner(q):
        to_wide(
            slot(packed, q, 1 - rail), near[q].at[local], send1.at[q], recv1.at[q],
            4 * side + inner_at + 1 - rail,
        ).start()
        pltpu.make_async_copy(slot(packed, q, rail), near[q].at[local], recv1.at[q]).start()

    def left(sems, q, count):
        rows = moved.at[pl.ds(0, count * part)]
        pltpu.make_async_copy(rows, rows, sems.at[q]).wait()

    def gather(q):
        @pl.when(outer)
        def _():
            if q >= WINDOW:
                left(send1, q - WINDOW, 2)
            start_outer(q)

        @pl.when(inner)
        def _():
            if q >= WINDOW:
                left(send1, q - WINDOW, 1)
            start_inner(q)

    for q in range(WINDOW):
        gather(q)

    def to_mate(src, dst, ssem, rsem):
        return pltpu.make_async_remote_copy(
            src_ref=src, dst_ref=dst, send_sem=ssem, recv_sem=rsem,
            device_id={"grad": mate}, device_id_type=MESH,
        )

    mine = pl.ds(pl.multiple_of(core * half, half), half)
    own_cols = pl.ds(pl.multiple_of(core * half, half), half)
    mate_cols = pl.ds(pl.multiple_of(mate * half, half), half)
    loads = [
        pltpu.make_async_copy(act.at[0, :, own_cols], a_own.at[mine], load_sem.at[0]),
        pltpu.make_async_copy(act.at[0, :, mate_cols], a_oth.at[mine], load_sem.at[1]),
        pltpu.make_async_copy(grad.at[0], g_own, load_sem.at[2]),
    ]
    swaps = [
        to_mate(act.at[0, :, mate_cols], a_own.at[mine], send_a.at[0], recv_a.at[0]),
        to_mate(act.at[0, :, own_cols], a_oth.at[mine], send_a.at[1], recv_a.at[1]),
        to_mate(grad.at[0], g_oth, send_g, recv_g),
    ]
    for c in loads + swaps:
        c.start()
    count = live[me]
    width = lhs_t.shape[0]
    scale = count.astype(jnp.float32)

    def factor_rows(i, carry):
        strip = pl.ds(pl.multiple_of(i * width, width), width)
        keep = lax.broadcasted_iota(jnp.int32, (2 * half, width), 0) < count
        tile = a_own[:, strip]
        lhs_t[...] = jnp.where(keep, tile, jnp.zeros_like(tile)).T

        def factor_cols(j, inner):
            span = pl.ds(pl.multiple_of(j * width, width), width)
            row = i * width + lax.broadcasted_iota(jnp.int32, (width, width), 0)
            col = j * width + lax.broadcasted_iota(jnp.int32, (width, width), 1)
            m_own[strip, span] = (
                dot(lhs_t[...], a_own[:, span]) / scale + jnp.where(row == col, DAMPING, 0.0)
            ).astype(jnp.bfloat16)
            m_oth[strip, span] = (dot(lhs_t[...], a_oth[:, span]) / scale).astype(jnp.bfloat16)
            return inner

        return lax.fori_loop(0, half // width, factor_cols, carry)

    def off_product(h, left, x):
        shift = pl.multiple_of(jnp.where(core == h, 0, quarter), quarter)
        return dot(left[h, :, :quarter], x[pl.ds(shift, quarter)]) + dot(
            left[h, :, quarter:], x[pl.ds(pl.multiple_of(quarter - shift, quarter), quarter)]
        )

    def cross(q):
        pltpu.make_async_copy(near[q], near[q], recv1.at[q]).wait()
        for i in range(many):
            stage_b[q * many + i] = near[q][route[4 * side + i]]
        to_wide(
            stage_b.at[pl.ds(q * many, many)], far[q], send2.at[q], recv2.at[q], across
        ).start()

    def deliver(q):
        pltpu.make_async_copy(far[q], far[q], recv2.at[q]).wait()
        for i in range(4):
            t = 4 * side + i
            crossed = jnp.full((part, LANES), route[8 + t], jnp.int32) != 0
            stage_c[4 * q + i] = jnp.where(
                crossed, far[q][route[24 + t]], near[q][route[16 + t]]
            )
        pltpu.make_async_copy(
            stage_c.at[4 * q + inner_at + rail], slot(moved, q, rail), recv3.at[q]
        ).start()
        to_wide(
            stage_c.at[4 * q + inner_at + 1 - rail], slot(moved, q, rail), send3.at[q], recv3.at[q],
            4 * side + inner_at + 1 - rail,
        ).start()
        to_wide(
            stage_c.at[4 * q + outer_at + 1 - rail], relay[q], send3.at[q], recv4.at[q],
            4 * side + outer_at + rail,
        ).start()
        to_wide(
            stage_c.at[4 * q + outer_at + rail], slot(moved, q, rail), send3.at[q], recv3.at[q],
            4 * side + outer_at + rail,
        ).start()

    def pass_on(q):
        pltpu.make_async_copy(relay[q], relay[q], recv4.at[q]).wait()
        to_wide(
            relay[q], slot(moved, q, rail), send4.at[q], recv3.at[q],
            4 * side + outer_at + 1 - rail,
        ).start()

    off = to_mate(moved.at[pl.ds(0, o_rows)], o_in, send_o, recv_o)
    off_at = -(-o_rows // (2 * part)) - 1

    def finish_off():
        off.wait()
        for h in range(2):
            other = jnp.where(mate == h, 0, o_rows // 2)
            for b in range(quarter // LANES):
                at = pl.multiple_of(other + b * quarter, quarter)
                s_o[h, b * LANES : (b + 1) * LANES, quarter:] = o_in[pl.ds(at, quarter)].T
        for h in range(2):
            first[h * quarter : (h + 1) * quarter] = off_product(h, s_o, g_oth)

    def assemble(q, next_block):
        chunk = moved.at[pl.ds(2 * q * part, 2 * part)]
        pltpu.make_async_copy(chunk, chunk, recv3.at[q]).wait()
        if q == off_at:
            off.start()
            for h in range(2):
                for b in range(quarter // LANES):
                    s_o[h, :, b * LANES : (b + 1) * LANES] = moved[
                        pl.ds(h * o_rows // 2 + b * quarter, quarter)
                    ]
        if q == min(off_at + 1, STEPS - 1):
            finish_off()
        while next_block < blocks and base(next_block + 1) <= 2 * (q + 1) * part:
            k = next_block
            lanes = slice(k * LANES, (k + 1) * LANES)
            s_d[0 : (k + 1) * LANES, lanes] = moved[pl.ds(base(k), (k + 1) * LANES)]
            if k:
                s_d[lanes, 0 : k * LANES] = moved[pl.ds(base(k), k * LANES)].T
            next_block += 1
        return next_block

    next_block, strips = 0, half // width
    for step in range(STEPS + LAG + 1):
        if step + WINDOW < STEPS:
            gather(step + WINDOW)
        if step < STEPS:
            pl.when(inner)(functools.partial(cross, step))
        if 1 <= step <= STEPS:
            pl.when(inner)(functools.partial(deliver, step - 1))
        if LAG <= step < STEPS + LAG:
            pl.when(outer)(functools.partial(pass_on, step - LAG))
        if step == 1:
            for c in loads + swaps:
                c.wait()
        if 1 <= step <= strips:
            factor_rows(step - 1, 0)
        if LAG < step:
            next_block = assemble(step - LAG - 1, next_block)

    tiles = [slice(i, i + width) for i in range(0, half, width)]
    for rows in tiles:
        first[rows] = first[rows] + dot(s_d[rows], g_own[...])
        f_own[rows] = first[rows].astype(jnp.bfloat16)
    swap = to_mate(f_own, f_oth, send_f, recv_f)
    swap.start()
    for rows in tiles:
        acc[rows] = dot(m_own[rows], f_own[...])
    swap.wait()
    for rows in tiles:
        c_own[rows] = (acc[rows] + dot(m_oth[rows], f_oth[...])).astype(jnp.bfloat16)
    swap = to_mate(c_own, c_oth, send_c, recv_c)
    swap.start()
    for rows in tiles:
        acc[rows] = 2.0 * first[rows] - dot(s_d[rows], c_own[...])
    swap.wait()
    for h in range(2):
        rows = slice(h * quarter, (h + 1) * quarter)
        out[0, rows] = (acc[rows] - off_product(h, s_o, c_oth)).astype(jnp.bfloat16)

    @pl.when(outer)
    def _():
        for q in range(STEPS):
            if q >= STEPS - WINDOW:
                left(send1, q, 2)
            left(send4, q, 1)

    @pl.when(inner)
    def _():
        for q in range(STEPS):
            if q >= STEPS - WINDOW:
                left(send1, q, 1)
            left(send2, q, many)
            left(send3, q, 3)


def run(n, many, operands):
    table, live_rows, activations, inverse, gradients = operands
    half, order = inverse.shape[1:]
    cols = gradients.shape[2]
    quarter = half // 2
    blocks = half // LANES
    o_rows = 2 * quarter * (quarter // LANES)
    used = o_rows + LANES * (blocks * (blocks + 1) // 2)
    pieces = n * CHUNKS if many is None else 2 * STEPS
    part = -(-used // (16 * pieces)) * 16
    full = part * pieces
    bf16, f32 = jnp.bfloat16, jnp.float32
    dma = pltpu.SemaphoreType.DMA
    vmem = pltpu.VMEM
    pack_count = 2 * (quarter // LANES) + blocks
    if many is None:
        stages = [vmem((pieces, part, LANES), bf16)]
    else:
        stages = [vmem((k * STEPS, part, LANES), bf16) for k in (many, 4)]
    scratch = [
        vmem((full, LANES), bf16),
        *stages,
        vmem((full, LANES), bf16),
        vmem((o_rows, LANES), bf16),
        vmem((order, half), bf16),
        vmem((order, half), bf16),
        vmem((256, order), bf16),
        vmem((half, half), bf16),
        vmem((half, half), bf16),
        vmem((half, half), bf16),
        vmem((2, quarter, half), bf16),
        vmem((half, cols), bf16),
        vmem((half, cols), bf16),
        vmem((half, cols), f32),
        vmem((half, cols), f32),
        vmem((half, cols), bf16),
        vmem((half, cols), bf16),
        vmem((half, cols), bf16),
        vmem((half, cols), bf16),
    ]
    if many is None:
        body = functools.partial(kernel, n, half, cols, part)
        scratch += [vmem((n, part, LANES), bf16) for _ in range(CHUNKS)]
        chunk_sems = [dma((CHUNKS,)) for _ in range(4)]
    else:
        body = functools.partial(line_kernel, n, half, cols, part, many)
        scratch += [vmem((4, part, LANES), bf16) for _ in range(STEPS)]
        scratch += [vmem((many, part, LANES), bf16) for _ in range(STEPS)]
        scratch += [vmem((part, LANES), bf16) for _ in range(STEPS)]
        chunk_sems = [dma((STEPS,)) for _ in range(8)]
    scratch += [dma((pack_count,)), dma((3,))]
    scratch += chunk_sems
    scratch += [dma((2,)), dma((2,))] + [dma(()) for _ in range(8)]
    smem = pl.BlockSpec(memory_space=pltpu.SMEM)
    hbm = pl.BlockSpec(memory_space=pl.ANY)
    return pl.pallas_call(
        body,
        out_shape=jax.ShapeDtypeStruct(gradients.shape, bf16),
        in_specs=[smem, smem, hbm, hbm, hbm],
        out_specs=pl.BlockSpec(memory_space=pltpu.VMEM),
        scratch_shapes=scratch,
        cost_estimate=pl.CostEstimate(
            flops=2 * half * order * (order + 3 * cols),
            bytes_accessed=4 * half * order + 4 * half * cols,
            transcendentals=0,
        ),
        compiler_params=pltpu.CompilerParams(
            collective_id=many or 0, has_side_effects=True, vmem_limit_bytes=56 * 1024 * 1024
        ),
    )(table, live_rows, activations, inverse, gradients)


def per_device(activations, inverse, gradients, matching, live_rows):
    n = lax.axis_size("wide")
    places = jnp.arange(n, dtype=jnp.int32)
    sources = jnp.sum(jnp.where(matching[None, :] == places[:, None], places[None, :], 0), axis=1)
    if n != 8:
        return run(n, None, (sources, live_rows, activations, inverse, gradients))
    side = places // 4
    cross = matching // 4 != side
    earlier = (side[None, :] == side[:, None]) & (places[None, :] < places[:, None])
    rank = jnp.sum(jnp.where(earlier & cross[None, :], 1, 0), axis=1)
    wanted = (side[None, :] == side[:, None]) & cross[None, :] & (
        rank[None, :] == (places % 4)[:, None]
    )
    leaving = jnp.sum(jnp.where(wanted, (places % 4)[None, :], 0), axis=1)
    comes = sources // 4 != side
    from_rank = jnp.sum(
        jnp.where((matching[None, :] == places[:, None]) & cross[None, :], rank[None, :], 0), axis=1
    )
    route = jnp.concatenate([leaving, comes.astype(jnp.int32), sources % 4, from_rank])
    many = jnp.sum(jnp.where(cross & (side == 0), 1, 0)).reshape(1)
    doms = lax.axis_size("dom")
    most, passed = many, many
    for _ in range(doms - 1):
        passed = lax.ppermute(passed, "dom", [(d, (d + 1) % doms) for d in range(doms)])
        most = jnp.maximum(most, passed)
    return lax.switch(
        jnp.clip(most[0] - 2, 0, 2),
        [functools.partial(run, n, k) for k in (2, 3, 4)],
        (route.astype(jnp.int32), live_rows, activations, inverse, gradients),
    )


def solution(mesh):
    return jax.shard_map(
        per_device,
        mesh=mesh,
        in_specs=(
            P(("dom", "wide"), "grad", None),
            P(("dom", "wide"), "grad", None),
            P(("dom", "wide"), "grad", None),
            P("dom"),
            P("dom"),
        ),
        out_specs=P(("dom", "wide"), "grad", None),
        check_vma=False,
    )
```

```python
import functools

import jax
import jax.numpy as jnp
from jax import lax
from jax.experimental import pallas as pl
from jax.experimental.pallas import tpu as pltpu
from jax.sharding import PartitionSpec as P

DAMPING = 1.0
LANES = 128
CHUNKS = 8
MESH = pl.DeviceIdType.MESH


def dot(a, b):
    return jnp.dot(a, b, preferred_element_type=jnp.float32)


def kernel(
    n, half, cols, parts,
    sources, live, act, inv, grad, out,
    packed, moved, o_in, a_own, a_oth, lhs_t, m_own, m_oth,
    s_d, s_o, g_own, g_oth, first, acc, f_own, f_oth, c_own, c_oth,
    *rest,
):
    chunks = len(parts)
    starts = [n * sum(parts[:q]) for q in range(chunks + 1)]
    arrived, stage = rest[:chunks], rest[chunks : 2 * chunks]
    (pack_sem, load_sem, send1, recv1, send2, recv2,
     send_a, recv_a, send_g, recv_g, send_o, recv_o, send_f, recv_f, send_c, recv_c) = rest[2 * chunks :]
    me = lax.axis_index("wide")
    core = lax.axis_index("grad")
    mate = 1 - core
    quarter = half // 2
    blocks = half // LANES
    o_rows = 2 * quarter * (quarter // LANES)

    def base(k):
        return o_rows + LANES * (k * (k + 1) // 2)

    barrier = pltpu.get_barrier_semaphore()

    copies = []
    for h in range(2):
        shift = jnp.where(core == h, 0, quarter)
        for b in range(quarter // LANES):
            source = pl.multiple_of(mate * half + shift + b * LANES, LANES)
            copies.append((
                inv.at[0, pl.ds(h * quarter, quarter), pl.ds(source, LANES)],
                packed.at[pl.ds(h * o_rows // 2 + b * quarter, quarter)],
            ))
    for k in range(blocks):
        source = pl.multiple_of(core * half + k * LANES, LANES)
        copies.append((
            inv.at[0, pl.ds(0, (k + 1) * LANES), pl.ds(source, LANES)],
            packed.at[pl.ds(base(k), (k + 1) * LANES)],
        ))
    copies = [pltpu.make_async_copy(s, d, pack_sem.at[i]) for i, (s, d) in enumerate(copies)]
    for c in copies:
        c.start()

    def greet(step, carry):
        pl.semaphore_signal(
            barrier, inc=1, device_id={"wide": lax.rem(me + step, n)}, device_id_type=MESH
        )
        return carry

    lax.fori_loop(1, n, greet, 0)
    pl.semaphore_signal(barrier, inc=1, device_id={"grad": mate}, device_id_type=MESH)
    pl.semaphore_wait(barrier, n)

    for c in copies:
        c.wait()

    for q in range(chunks):
        def scatter(step, carry, q=q):
            peer = lax.rem(me + step, n)
            pltpu.make_async_remote_copy(
                src_ref=packed.at[pl.ds(pl.multiple_of(starts[q] + peer * parts[q], 16), parts[q])],
                dst_ref=arrived[q].at[me],
                send_sem=send1.at[q],
                recv_sem=recv1.at[q],
                device_id={"wide": peer},
                device_id_type=MESH,
            ).start()
            return carry

        lax.fori_loop(1, n, scatter, 0)
        pltpu.make_async_copy(
            packed.at[pl.ds(pl.multiple_of(starts[q] + me * parts[q], 16), parts[q])],
            arrived[q].at[me],
            recv1.at[q],
        ).start()

    def to_mate(src, dst, ssem, rsem):
        return pltpu.make_async_remote_copy(
            src_ref=src, dst_ref=dst, send_sem=ssem, recv_sem=rsem,
            device_id={"grad": mate}, device_id_type=MESH,
        )

    mine = pl.ds(pl.multiple_of(core * half, half), half)
    own_cols = pl.ds(pl.multiple_of(core * half, half), half)
    mate_cols = pl.ds(pl.multiple_of(mate * half, half), half)
    loads = [
        pltpu.make_async_copy(act.at[0, :, own_cols], a_own.at[mine], load_sem.at[0]),
        pltpu.make_async_copy(act.at[0, :, mate_cols], a_oth.at[mine], load_sem.at[1]),
        pltpu.make_async_copy(grad.at[0], g_own, load_sem.at[2]),
    ]
    swaps = [
        to_mate(act.at[0, :, mate_cols], a_own.at[mine], send_a.at[0], recv_a.at[0]),
        to_mate(act.at[0, :, own_cols], a_oth.at[mine], send_a.at[1], recv_a.at[1]),
        to_mate(grad.at[0], g_oth, send_g, recv_g),
    ]
    for c in loads + swaps:
        c.start()
    for c in loads:
        c.wait()
    for c in swaps:
        c.wait()

    count = live[me]
    width = lhs_t.shape[0]
    scale = count.astype(jnp.float32)

    def factor_rows(i, carry):
        strip = pl.ds(pl.multiple_of(i * width, width), width)
        keep = lax.broadcasted_iota(jnp.int32, (2 * half, width), 0) < count
        tile = a_own[:, strip]
        lhs_t[...] = jnp.where(keep, tile, jnp.zeros_like(tile)).T

        def factor_cols(j, inner):
            span = pl.ds(pl.multiple_of(j * width, width), width)
            row = i * width + lax.broadcasted_iota(jnp.int32, (width, width), 0)
            col = j * width + lax.broadcasted_iota(jnp.int32, (width, width), 1)
            m_own[strip, span] = (
                dot(lhs_t[...], a_own[:, span]) / scale + jnp.where(row == col, DAMPING, 0.0)
            ).astype(jnp.bfloat16)
            m_oth[strip, span] = (dot(lhs_t[...], a_oth[:, span]) / scale).astype(jnp.bfloat16)
            return inner

        return lax.fori_loop(0, half // width, factor_cols, carry)

    lax.fori_loop(0, half // width, factor_rows, 0)

    for q in range(chunks):
        pltpu.make_async_copy(arrived[q], arrived[q], recv1.at[q]).wait()

        def choose(t, carry, q=q):
            stage[q][t] = arrived[q][sources[t]]
            return carry

        lax.fori_loop(0, n, choose, 0)
        landing = pl.ds(pl.multiple_of(starts[q] + me * parts[q], 16), parts[q])

        def deliver(step, carry, q=q, landing=landing):
            peer = lax.rem(me + step, n)
            pltpu.make_async_remote_copy(
                src_ref=stage[q].at[peer],
                dst_ref=moved.at[landing],
                send_sem=send2.at[q],
                recv_sem=recv2.at[q],
                device_id={"wide": peer},
                device_id_type=MESH,
            ).start()
            return carry

        lax.fori_loop(1, n, deliver, 0)
        pltpu.make_async_copy(stage[q].at[me], moved.at[landing], recv2.at[q]).start()

    def off_product(h, left, x):
        shift = pl.multiple_of(jnp.where(core == h, 0, quarter), quarter)
        return dot(left[h, :, :quarter], x[pl.ds(shift, quarter)]) + dot(
            left[h, :, quarter:], x[pl.ds(pl.multiple_of(quarter - shift, quarter), quarter)]
        )

    off = to_mate(moved.at[pl.ds(0, o_rows)], o_in, send_o, recv_o)
    off_at, next_block = None, 0
    for q in range(chunks):
        chunk = moved.at[pl.ds(starts[q], n * parts[q])]
        pltpu.make_async_copy(chunk, chunk, recv2.at[q]).wait()
        end = starts[q + 1]
        if off_at is None and end >= o_rows:
            off_at = q
            off.start()
            for h in range(2):
                for b in range(quarter // LANES):
                    s_o[h, :, b * LANES : (b + 1) * LANES] = moved[
                        pl.ds(h * o_rows // 2 + b * quarter, quarter)
                    ]
            off.wait()
            for h in range(2):
                other = jnp.where(mate == h, 0, o_rows // 2)
                for b in range(quarter // LANES):
                    at = pl.multiple_of(other + b * quarter, quarter)
                    s_o[h, b * LANES : (b + 1) * LANES, quarter:] = o_in[pl.ds(at, quarter)].T
            for h in range(2):
                first[h * quarter : (h + 1) * quarter] = off_product(h, s_o, g_oth)
        while off_at is not None and next_block < blocks and base(next_block + 1) <= end:
            k = next_block
            lanes = slice(k * LANES, (k + 1) * LANES)
            s_d[0 : (k + 1) * LANES, lanes] = moved[pl.ds(base(k), (k + 1) * LANES)]
            if k:
                s_d[lanes, 0 : k * LANES] = moved[pl.ds(base(k), k * LANES)].T
            next_block += 1

    tiles = [slice(i, i + width) for i in range(0, half, width)]
    for rows in tiles:
        first[rows] = first[rows] + dot(s_d[rows], g_own[...])
        f_own[rows] = first[rows].astype(jnp.bfloat16)
    swap = to_mate(f_own, f_oth, send_f, recv_f)
    swap.start()
    for rows in tiles:
        acc[rows] = dot(m_own[rows], f_own[...])
    swap.wait()
    for rows in tiles:
        c_own[rows] = (acc[rows] + dot(m_oth[rows], f_oth[...])).astype(jnp.bfloat16)
    swap = to_mate(c_own, c_oth, send_c, recv_c)
    swap.start()
    for rows in tiles:
        acc[rows] = 2.0 * first[rows] - dot(s_d[rows], c_own[...])
    swap.wait()
    for h in range(2):
        rows = slice(h * quarter, (h + 1) * quarter)
        out[0, rows] = (acc[rows] - off_product(h, s_o, c_oth)).astype(jnp.bfloat16)

    for q in range(chunks):
        sent = moved.at[pl.ds(0, (n - 1) * parts[q])]
        pltpu.make_async_copy(sent, sent, send1.at[q]).wait()
        pltpu.make_async_copy(sent, sent, send2.at[q]).wait()


def per_device(activations, inverse, gradients, matching, live_rows):
    n = lax.axis_size("wide")
    half, order = inverse.shape[1:]
    cols = gradients.shape[2]
    places = jnp.arange(n, dtype=jnp.int32)
    sources = jnp.sum(jnp.where(matching[None, :] == places[:, None], places[None, :], 0), axis=1)
    quarter = half // 2
    blocks = half // LANES
    o_rows = 2 * quarter * (quarter // LANES)
    used = o_rows + LANES * (blocks * (blocks + 1) // 2)
    units = -(-used // (16 * n))
    per = -(-units // CHUNKS)
    parts = [16 * min(per, units - at) for at in range(0, units, per)]
    full = 16 * n * units
    bf16, f32 = jnp.bfloat16, jnp.float32
    dma = pltpu.SemaphoreType.DMA
    vmem = pltpu.VMEM
    pack_count = 2 * (quarter // LANES) + blocks
    scratch = [
        vmem((full, LANES), bf16),
        vmem((full, LANES), bf16),
        vmem((o_rows, LANES), bf16),
        vmem((order, half), bf16),
        vmem((order, half), bf16),
        vmem((256, order), bf16),
        vmem((half, half), bf16),
        vmem((half, half), bf16),
        vmem((half, half), bf16),
        vmem((2, quarter, half), bf16),
        vmem((half, cols), bf16),
        vmem((half, cols), bf16),
        vmem((half, cols), f32),
        vmem((half, cols), f32),
        vmem((half, cols), bf16),
        vmem((half, cols), bf16),
        vmem((half, cols), bf16),
        vmem((half, cols), bf16),
    ]
    scratch += 2 * [vmem((n, part, LANES), bf16) for part in parts]
    scratch += [dma((pack_count,)), dma((3,))]
    scratch += [dma((len(parts),)) for _ in range(4)]
    scratch += [dma((2,)), dma((2,))] + [dma(()) for _ in range(8)]
    smem = pl.BlockSpec(memory_space=pltpu.SMEM)
    hbm = pl.BlockSpec(memory_space=pl.ANY)
    return pl.pallas_call(
        functools.partial(kernel, n, half, cols, parts),
        out_shape=jax.ShapeDtypeStruct(gradients.shape, bf16),
        in_specs=[smem, smem, hbm, hbm, hbm],
        out_specs=pl.BlockSpec(memory_space=pltpu.VMEM),
        scratch_shapes=scratch,
        cost_estimate=pl.CostEstimate(
            flops=2 * half * order * (order + 3 * cols),
            bytes_accessed=4 * half * order + 4 * half * cols,
            transcendentals=0,
        ),
        compiler_params=pltpu.CompilerParams(
            collective_id=0, has_side_effects=True, vmem_limit_bytes=56 * 1024 * 1024
        ),
    )(sources, live_rows, activations, inverse, gradients)


def solution(mesh):
    return jax.shard_map(
        per_device,
        mesh=mesh,
        in_specs=(
            P(("dom", "wide"), "grad", None),
            P(("dom", "wide"), "grad", None),
            P(("dom", "wide"), "grad", None),
            P("dom"),
            P("dom"),
        ),
        out_specs=P(("dom", "wide"), "grad", None),
        check_vma=False,
    )
```

```python
import functools

import jax
import jax.numpy as jnp
from jax import lax
from jax.experimental import pallas as pl
from jax.experimental.pallas import tpu as pltpu
from jax.sharding import PartitionSpec as P

DAMPING = 1.0
LANES = 128
CHUNKS = 4
MESH = pl.DeviceIdType.MESH


def dot(a, b):
    return jnp.dot(a, b, preferred_element_type=jnp.float32)


def kernel(
    n, half, cols, part,
    sources, live, act, inv, grad, out,
    packed, stage, moved, o_in, a_own, a_oth, lhs_t, m_own, m_oth,
    s_d, s_o, g_own, g_oth, first, acc, f_own, f_oth, c_own, c_oth,
    *rest,
):
    arrived = rest[:CHUNKS]
    (pack_sem, load_sem, send1, recv1, send2, recv2,
     send_a, recv_a, send_g, recv_g, send_o, recv_o, send_f, recv_f, send_c, recv_c) = rest[CHUNKS:]
    me = lax.axis_index("wide")
    core = lax.axis_index("grad")
    mate = 1 - core
    quarter = half // 2
    blocks = half // LANES
    o_rows = 2 * quarter * (quarter // LANES)

    def base(k):
        return o_rows + LANES * (k * (k + 1) // 2)

    barrier = pltpu.get_barrier_semaphore()

    copies = []
    for h in range(2):
        shift = jnp.where(core == h, 0, quarter)
        for b in range(quarter // LANES):
            source = pl.multiple_of(mate * half + shift + b * LANES, LANES)
            copies.append((
                inv.at[0, pl.ds(h * quarter, quarter), pl.ds(source, LANES)],
                packed.at[pl.ds(h * o_rows // 2 + b * quarter, quarter)],
            ))
    for k in range(blocks):
        source = pl.multiple_of(core * half + k * LANES, LANES)
        copies.append((
            inv.at[0, pl.ds(0, (k + 1) * LANES), pl.ds(source, LANES)],
            packed.at[pl.ds(base(k), (k + 1) * LANES)],
        ))
    copies = [pltpu.make_async_copy(s, d, pack_sem.at[i]) for i, (s, d) in enumerate(copies)]
    for c in copies:
        c.start()

    def greet(step, carry):
        pl.semaphore_signal(
            barrier, inc=1, device_id={"wide": lax.rem(me + step, n)}, device_id_type=MESH
        )
        return carry

    lax.fori_loop(1, n, greet, 0)
    pl.semaphore_signal(barrier, inc=1, device_id={"grad": mate}, device_id_type=MESH)
    pl.semaphore_wait(barrier, n)

    begins = [h * o_rows // 2 + b * quarter for h in range(2) for b in range(quarter // LANES)]
    begins += [base(k) for k in range(blocks)]
    waited = 0
    for q in range(CHUNKS):
        while waited < len(copies) and (begins[waited] < (q + 1) * n * part or q == CHUNKS - 1):
            copies[waited].wait()
            waited += 1

        def scatter(step, carry, q=q):
            peer = lax.rem(me + step, n)
            pltpu.make_async_remote_copy(
                src_ref=packed.at[pl.ds(pl.multiple_of((q * n + peer) * part, 16), part)],
                dst_ref=arrived[q].at[me],
                send_sem=send1.at[q],
                recv_sem=recv1.at[q],
                device_id={"wide": peer},
                device_id_type=MESH,
            ).start()
            return carry

        lax.fori_loop(1, n, scatter, 0)
        pltpu.make_async_copy(
            packed.at[pl.ds(pl.multiple_of((q * n + me) * part, 16), part)],
            arrived[q].at[me],
            recv1.at[q],
        ).start()

    def to_mate(src, dst, ssem, rsem):
        return pltpu.make_async_remote_copy(
            src_ref=src, dst_ref=dst, send_sem=ssem, recv_sem=rsem,
            device_id={"grad": mate}, device_id_type=MESH,
        )

    mine = pl.ds(pl.multiple_of(core * half, half), half)
    own_cols = pl.ds(pl.multiple_of(core * half, half), half)
    mate_cols = pl.ds(pl.multiple_of(mate * half, half), half)
    loads = [
        pltpu.make_async_copy(act.at[0, :, own_cols], a_own.at[mine], load_sem.at[0]),
        pltpu.make_async_copy(act.at[0, :, mate_cols], a_oth.at[mine], load_sem.at[1]),
        pltpu.make_async_copy(grad.at[0], g_own, load_sem.at[2]),
    ]
    swaps = [
        to_mate(act.at[0, :, mate_cols], a_own.at[mine], send_a.at[0], recv_a.at[0]),
        to_mate(act.at[0, :, own_cols], a_oth.at[mine], send_a.at[1], recv_a.at[1]),
        to_mate(grad.at[0], g_oth, send_g, recv_g),
    ]
    for c in loads + swaps:
        c.start()
    for c in loads:
        c.wait()
    for c in swaps:
        c.wait()

    count = live[me]
    width = lhs_t.shape[0]
    scale = count.astype(jnp.float32)

    def factor_rows(i, carry):
        strip = pl.ds(pl.multiple_of(i * width, width), width)
        keep = lax.broadcasted_iota(jnp.int32, (2 * half, width), 0) < count
        tile = a_own[:, strip]
        lhs_t[...] = jnp.where(keep, tile, jnp.zeros_like(tile)).T

        def factor_cols(j, inner):
            span = pl.ds(pl.multiple_of(j * width, width), width)
            row = i * width + lax.broadcasted_iota(jnp.int32, (width, width), 0)
            col = j * width + lax.broadcasted_iota(jnp.int32, (width, width), 1)
            m_own[strip, span] = (
                dot(lhs_t[...], a_own[:, span]) / scale + jnp.where(row == col, DAMPING, 0.0)
            ).astype(jnp.bfloat16)
            m_oth[strip, span] = (dot(lhs_t[...], a_oth[:, span]) / scale).astype(jnp.bfloat16)
            return inner

        return lax.fori_loop(0, half // width, factor_cols, carry)

    lax.fori_loop(0, half // width, factor_rows, 0)

    for q in range(CHUNKS):
        pltpu.make_async_copy(arrived[q], arrived[q], recv1.at[q]).wait()

        def choose(t, carry, q=q):
            stage[q * n + t] = arrived[q][sources[t]]
            return carry

        lax.fori_loop(0, n, choose, 0)
        landing = pl.ds(pl.multiple_of((q * n + me) * part, 16), part)

        def deliver(step, carry, q=q, landing=landing):
            peer = lax.rem(me + step, n)
            pltpu.make_async_remote_copy(
                src_ref=stage.at[q * n + peer],
                dst_ref=moved.at[landing],
                send_sem=send2.at[q],
                recv_sem=recv2.at[q],
                device_id={"wide": peer},
                device_id_type=MESH,
            ).start()
            return carry

        lax.fori_loop(1, n, deliver, 0)
        pltpu.make_async_copy(stage.at[q * n + me], moved.at[landing], recv2.at[q]).start()

    def off_product(h, left, x):
        shift = pl.multiple_of(jnp.where(core == h, 0, quarter), quarter)
        return dot(left[h, :, :quarter], x[pl.ds(shift, quarter)]) + dot(
            left[h, :, quarter:], x[pl.ds(pl.multiple_of(quarter - shift, quarter), quarter)]
        )

    off = to_mate(moved.at[pl.ds(0, o_rows)], o_in, send_o, recv_o)
    off_at, next_block = None, 0
    for q in range(CHUNKS):
        chunk = moved.at[pl.ds(q * n * part, n * part)]
        pltpu.make_async_copy(chunk, chunk, recv2.at[q]).wait()
        end = (q + 1) * n * part
        if off_at is None and end >= o_rows:
            off_at = q
            off.start()
            for h in range(2):
                for b in range(quarter // LANES):
                    s_o[h, :, b * LANES : (b + 1) * LANES] = moved[
                        pl.ds(h * o_rows // 2 + b * quarter, quarter)
                    ]
            off.wait()
            for h in range(2):
                other = jnp.where(mate == h, 0, o_rows // 2)
                for b in range(quarter // LANES):
                    at = pl.multiple_of(other + b * quarter, quarter)
                    s_o[h, b * LANES : (b + 1) * LANES, quarter:] = o_in[pl.ds(at, quarter)].T
            for h in range(2):
                first[h * quarter : (h + 1) * quarter] = off_product(h, s_o, g_oth)
        while off_at is not None and next_block < blocks and base(next_block + 1) <= end:
            k = next_block
            lanes = slice(k * LANES, (k + 1) * LANES)
            s_d[0 : (k + 1) * LANES, lanes] = moved[pl.ds(base(k), (k + 1) * LANES)]
            if k:
                s_d[lanes, 0 : k * LANES] = moved[pl.ds(base(k), k * LANES)].T
            next_block += 1

    tiles = [slice(i, i + width) for i in range(0, half, width)]
    for rows in tiles:
        first[rows] = first[rows] + dot(s_d[rows], g_own[...])
        f_own[rows] = first[rows].astype(jnp.bfloat16)
    swap = to_mate(f_own, f_oth, send_f, recv_f)
    swap.start()
    for rows in tiles:
        acc[rows] = dot(m_own[rows], f_own[...])
    swap.wait()
    for rows in tiles:
        c_own[rows] = (acc[rows] + dot(m_oth[rows], f_oth[...])).astype(jnp.bfloat16)
    swap = to_mate(c_own, c_oth, send_c, recv_c)
    swap.start()
    for rows in tiles:
        acc[rows] = 2.0 * first[rows] - dot(s_d[rows], c_own[...])
    swap.wait()
    for h in range(2):
        rows = slice(h * quarter, (h + 1) * quarter)
        out[0, rows] = (acc[rows] - off_product(h, s_o, c_oth)).astype(jnp.bfloat16)

    for q in range(CHUNKS):
        sent = moved.at[pl.ds(0, (n - 1) * part)]
        pltpu.make_async_copy(sent, sent, send1.at[q]).wait()
        pltpu.make_async_copy(sent, sent, send2.at[q]).wait()


def per_device(activations, inverse, gradients, matching, live_rows):
    n = lax.axis_size("wide")
    half, order = inverse.shape[1:]
    cols = gradients.shape[2]
    places = jnp.arange(n, dtype=jnp.int32)
    sources = jnp.sum(jnp.where(matching[None, :] == places[:, None], places[None, :], 0), axis=1)
    quarter = half // 2
    blocks = half // LANES
    o_rows = 2 * quarter * (quarter // LANES)
    used = o_rows + LANES * (blocks * (blocks + 1) // 2)
    part = -(-used // (16 * n * CHUNKS)) * 16
    full = part * n * CHUNKS
    bf16, f32 = jnp.bfloat16, jnp.float32
    dma = pltpu.SemaphoreType.DMA
    vmem = pltpu.VMEM
    pack_count = 2 * (quarter // LANES) + blocks
    scratch = [
        vmem((full, LANES), bf16),
        vmem((CHUNKS * n, part, LANES), bf16),
        vmem((full, LANES), bf16),
        vmem((o_rows, LANES), bf16),
        vmem((order, half), bf16),
        vmem((order, half), bf16),
        vmem((256, order), bf16),
        vmem((half, half), bf16),
        vmem((half, half), bf16),
        vmem((half, half), bf16),
        vmem((2, quarter, half), bf16),
        vmem((half, cols), bf16),
        vmem((half, cols), bf16),
        vmem((half, cols), f32),
        vmem((half, cols), f32),
        vmem((half, cols), bf16),
        vmem((half, cols), bf16),
        vmem((half, cols), bf16),
        vmem((half, cols), bf16),
    ]
    scratch += [vmem((n, part, LANES), bf16) for _ in range(CHUNKS)]
    scratch += [dma((pack_count,)), dma((3,))]
    scratch += [dma((CHUNKS,)) for _ in range(4)]
    scratch += [dma((2,)), dma((2,))] + [dma(()) for _ in range(8)]
    smem = pl.BlockSpec(memory_space=pltpu.SMEM)
    hbm = pl.BlockSpec(memory_space=pl.ANY)
    return pl.pallas_call(
        functools.partial(kernel, n, half, cols, part),
        out_shape=jax.ShapeDtypeStruct(gradients.shape, bf16),
        in_specs=[smem, smem, hbm, hbm, hbm],
        out_specs=pl.BlockSpec(memory_space=pltpu.VMEM),
        scratch_shapes=scratch,
        cost_estimate=pl.CostEstimate(
            flops=2 * half * order * (order + 3 * cols),
            bytes_accessed=4 * half * order + 4 * half * cols,
            transcendentals=0,
        ),
        compiler_params=pltpu.CompilerParams(
            collective_id=0, has_side_effects=True, vmem_limit_bytes=56 * 1024 * 1024
        ),
    )(sources, live_rows, activations, inverse, gradients)


def solution(mesh):
    return jax.shard_map(
        per_device,
        mesh=mesh,
        in_specs=(
            P(("dom", "wide"), "grad", None),
            P(("dom", "wide"), "grad", None),
            P(("dom", "wide"), "grad", None),
            P("dom"),
            P("dom"),
        ),
        out_specs=P(("dom", "wide"), "grad", None),
        check_vma=False,
    )
```
